128 devices in a mesh: frame: 16 (over y, x), orbit: 8 (over z, core).
Axes of the slice: x: 4, y: 4, z: 4, core: 2. Of those that a mesh axis runs over, the one named last changes fastest.
Arguments:
- tokens: bfloat16 [65536, 1536], P(('orbit', 'frame')), parts along dimension 0, may hold values from -8 to 8
- keep_count: int32 [128], P('orbit'), parts along dimension 0, may hold values from 1 to 3, 32 in all
- keep_order: int32 [128, 4], P(('orbit', 'frame')), parts along dimension 0, may hold values from 0 to 3, each once within a row
- w_qkv: bfloat16 [1536, 4608], replicated, may hold values from -1 to 1
- w_out: bfloat16 [1536, 1536], replicated, may hold values from -0.15625 to 0.15625
Outputs:
- updated: bfloat16 [65536, 1536], P(('orbit', 'frame')), parts along dimension 0
The draws below stay inside these ranges and needn't reach their ends.
There are 8 independent parts, one for each index of `orbit`. The reference program is written for one: setup_inputs(seed, part) draws one part's arguments, and reference() takes and returns one part's arrays. A program takes and returns all parts, laid end to end along the dimension named above; an argument that names none is the same for every part. Nothing has to cross between parts.
Inputs may be any that keep to these rules, and one draw needn't show every extreme that they name: `keep_count`: the counts sum to 32 and some frame keeps exactly 3 blocks. `keep_order`: each row is a permutation of the numbers 0 to 3.
All inputs are finite; a program needn't handle non-finite values.
Results may differ from the reference program's by a relative error of at most 0.0086.
Values may be sent and summed in bfloat16 or wider, within the bound.
A program may use at most 320 MiB of HBM per device.

```python
import math
import jax
import jax.numpy as jnp
import numpy as np
from jax import lax

D = 1536
HEADS = 24
HEAD_DIM = 64
BLK = 128
KEEPB = 2
MOSTB = 3
TOKF = 512
NB = 4
HW = 1536
FRAMES = 16
TOKENS = 8192
N_FRAME = 16


def draw_tokens(key, part):
    key = jax.random.fold_in(key, 11)
    first = jax.random.fold_in(key, 0)
    values = jax.random.normal(first, (FRAMES, TOKF, D), jnp.float32)
    return jnp.clip(values, -8.0, 8.0).reshape(TOKENS, D).astype(jnp.bfloat16)


def draw_w_qkv(key, part):
    key = jax.random.fold_in(key, 23)
    first = jax.random.fold_in(key, 0)
    width = HEADS * HEAD_DIM
    values = jax.random.normal(first, (D, 3 * width), jnp.float32) * D ** (-0.5)
    return jnp.clip(values, -1.0, 1.0).astype(jnp.bfloat16)


def length_profile(amount, total, bound, lean):
    weights = [(1 << 20) // math.isqrt(rank ** lean) + 1 for rank in range(2, amount + 1)]
    surplus, counts = total - bound - (amount - 1), [1] * (amount - 1)
    while surplus > 0:
        candidates = [i for i in range(amount - 1) if counts[i] < bound]
        whole, remaining = sum([weights[i] for i in candidates]), surplus
        for i in candidates:
            addition = min(bound - counts[i], max(1, remaining * weights[i] // whole), surplus)
            counts[i] = counts[i] + addition
            surplus = surplus - addition
    return np.array([bound] + counts)


def uneven_parts(key, count, total, bound, lean):
    if count == 2:
        one = jax.random.randint(key, (), max(1, total - bound), min(bound, total - 1) + 1)
        return jnp.stack([one, total - one])
    tallies = jnp.asarray(length_profile(count, total, bound, lean), jnp.int32)
    pairs = (count - 1) // 2
    donor, receiver = tallies[1:1 + 2 * pairs:2], tallies[2:2 + 2 * pairs:2]
    margin = jnp.minimum(donor - 1, bound - receiver)
    passed = jax.random.randint(jax.random.fold_in(key, 1), (pairs,), 0, 1 << 20) % (margin + 1)
    tallies = tallies.at[1:1 + 2 * pairs:2].set(donor - passed).at[2:2 + 2 * pairs:2].set(receiver + passed)
    return tallies[jax.random.permutation(jax.random.fold_in(key, 2), count)]


def centred(rng, extent, scale, limit, kind=jnp.bfloat16):
    drawn = jax.random.normal(rng, extent, jnp.float32) * scale
    return jnp.minimum(jnp.maximum(drawn, -limit), limit).astype(kind)


def setup_inputs(seed: int = 0, part: int = 0) -> dict:
    streams_of = jax.random.split(jax.random.key(seed), 6)
    own_keys = jax.random.split(jax.random.fold_in(streams_of[5], part), 6)
    return {
        "tokens": draw_tokens(jax.random.fold_in(jax.random.fold_in(streams_of[5], part), 71), part),
        "keep_count": uneven_parts(own_keys[1], FRAMES, KEEPB * FRAMES, MOSTB, 2).astype(jnp.int32),
        "keep_order": jax.vmap(lambda own: jax.random.permutation(own, NB))(jax.random.split(own_keys[2], FRAMES)).reshape((FRAMES, NB)).astype(jnp.int32),
        "w_qkv": draw_w_qkv(jax.random.fold_in(streams_of[5], 71), part),
        "w_out": centred(streams_of[4], (HW, D), HW ** -0.5, 0.15625),
    }


def rms_rows(values):
    wide = values.astype(jnp.float32)
    return wide * lax.rsqrt(lax.optimization_barrier(jnp.mean(wide * wide, axis=-1, keepdims=True)) + 1e-06)

def frame_partial(query, keys, values, count):
    rows = query.shape[0]
    q_heads = query.reshape(rows, HEADS, HEAD_DIM).astype(jnp.float32)
    k_heads = keys.reshape(rows, HEADS, HEAD_DIM).astype(jnp.float32)
    v_heads = values.reshape(rows, HEADS, HEAD_DIM).astype(jnp.float32)
    scores = jnp.einsum('rhd,shd->rhs', q_heads, k_heads) * HEAD_DIM ** (-0.5)
    live = jnp.arange(rows, dtype=jnp.int32) < count * BLK
    scores = jnp.where(live[None, None, :], scores, jnp.float32(-1e+30))
    peak = lax.optimization_barrier(jnp.max(scores, axis=-1))
    weights = jnp.exp(scores - peak[..., None])
    total = lax.optimization_barrier(jnp.sum(weights, axis=-1))
    rounded = weights.astype(jnp.bfloat16).astype(jnp.float32)
    summed = jnp.einsum('rhs,shd->rhd', rounded, v_heads)
    return (peak, total, summed)

def reference(tokens, keep_count, keep_order, w_qkv, w_out):
    width = HEADS * HEAD_DIM
    rows = MOSTB * BLK
    nblocks = TOKF // BLK
    reach = N_FRAME // 4
    blocks = tokens.reshape(N_FRAME, nblocks, BLK, D)
    qkv_all = []
    for frame in range(N_FRAME):
        chosen = keep_order[frame, :MOSTB]
        kept = blocks[frame][chosen].reshape(rows, D)
        normed = rms_rows(kept).astype(jnp.bfloat16)
        qkv_all.append(jnp.dot(normed, w_qkv, preferred_element_type=jnp.float32).astype(jnp.bfloat16))
    results = []
    for frame in range(N_FRAME):
        query = qkv_all[frame][:, :width]
        peaks, totals, sums = ([], [], [])
        for offset in range(-reach, reach + 1):
            other = (frame + offset) % N_FRAME
            peak, total, summed = frame_partial(query, qkv_all[other][:, width:2 * width], qkv_all[other][:, 2 * width:], keep_count[other])
            peaks.append(peak)
            totals.append(total)
            sums.append(summed)
        peaks = jnp.stack(peaks)
        top = lax.optimization_barrier(jnp.max(peaks, axis=0))
        scale = jnp.exp(peaks - top[None])
        total = lax.optimization_barrier(jnp.sum(scale * jnp.stack(totals), axis=0))
        summed = lax.optimization_barrier(jnp.sum(scale[..., None] * jnp.stack(sums), axis=0))
        attended = (summed / total[..., None]).reshape(rows, width).astype(jnp.bfloat16)
        projected = jnp.dot(attended, w_out, preferred_element_type=jnp.float32)
        normalized = rms_rows(projected).astype(jnp.bfloat16)
        live_block = jnp.arange(MOSTB, dtype=jnp.int32) < keep_count[frame]
        placing = (keep_order[frame, :MOSTB][None, :] == jnp.arange(nblocks, dtype=jnp.int32)[:, None]) & live_block[None, :]
        placed = jnp.dot(placing.astype(jnp.bfloat16), normalized.reshape(MOSTB, BLK * D), preferred_element_type=jnp.float32)
        results.append(placed.astype(jnp.bfloat16).reshape(TOKF, D))
    return jnp.concatenate(results, axis=0)
```

```python
import functools

import jax
import jax.numpy as jnp
from jax import lax
from jax.experimental import pallas as pl
from jax.experimental.pallas import tpu as pltpu
from jax.sharding import PartitionSpec as P

D = 1536
HEADS = 24
HEAD_DIM = 64
BLK = 128
MOSTB = 3
ROWS = MOSTB * BLK
SIDE = 4
GW = 384
PAIRS = 3
CH = 512
NCH = 7
KROWS = 36 * BLK + CH
SCALE = HEAD_DIM ** (-0.5) * 1.4426950408889634
VMEM = 60 * 2**20
MESH = pl.DeviceIdType.MESH


def place():
    me = lax.axis_index("frame")
    return me // SIDE, me % SIDE


def device(y, x):
    return {"frame": (y % SIDE) * SIDE + x % SIDE}


def norm_kernel(order, tok, out):
    wide = tok[...].astype(jnp.float32)
    scale = lax.rsqrt(jnp.mean(wide * wide, axis=-1, keepdims=True) + 1e-06)
    out[...] = (wide * scale).astype(jnp.bfloat16)


def norm_kept(order_row, tokens):
    return pl.pallas_call(
        norm_kernel,
        grid_spec=pltpu.PrefetchScalarGridSpec(
            num_scalar_prefetch=1,
            grid=(MOSTB,),
            in_specs=[pl.BlockSpec((BLK, D), lambda j, order: (order[j], 0))],
            out_specs=pl.BlockSpec((BLK, D), lambda j, order: (j, 0)),
        ),
        out_shape=jax.ShapeDtypeStruct((ROWS, D), jnp.bfloat16),
        name="norm_kept",
    )(order_row, tokens)


BLOCKS = ((0, 1), (0, 2), (1, 1), (1, 2), (3, 1), (3, 2), (2, 1), (2, 2), (1, 0), (3, 0), (2, 0), (0, 0))


def exchange_kernel(normed, w, kv, q, wbuf, kvs, qs, wsem, xs, xr, qss, qsr, ys, yr):
    y, x = place()
    loads = []
    for i, (delta, kind) in enumerate(BLOCKS):
        col = pl.multiple_of(kind * (HEADS * HEAD_DIM) + ((x + delta) % SIDE) * GW, 128)
        load = pltpu.make_async_copy(w.at[:, pl.ds(col, GW)], wbuf.at[i], wsem.at[i])
        load.start()
        loads.append(load)
    barrier = pltpu.get_barrier_semaphore()
    peers = [(0, 1), (0, 2), (0, 3), (1, 0), (3, 0)]
    for dy, dx in peers:
        pl.semaphore_signal(barrier, inc=1, device_id=device(y + dy, x + dx), device_id_type=MESH)
    pl.semaphore_wait(barrier, len(peers))

    def product(i, put):
        loads[i].wait()

        def rows(r, carry):
            at = pl.ds(pl.multiple_of(r * BLK, BLK), BLK)
            value = jnp.dot(normed[at, :], wbuf[i], preferred_element_type=jnp.float32)
            put(at, value)
            return carry

        lax.fori_loop(0, MOSTB, rows, 0)

    def up_down(delta):
        frame = (x - delta) % SIDE
        copies = []
        for way, (dy, base) in enumerate(((1, 0), (-1, 2 * SIDE))):
            copy = pltpu.make_async_remote_copy(
                kv.at[SIDE + frame],
                kv.at[base + frame],
                ys.at[way, delta],
                yr.at[way, delta],
                device_id=device(y + dy, x),
                device_id_type=MESH,
            )
            copy.start()
            copies.append(copy)
        return copies

    sent = []
    across = {}
    for i, (delta, kind) in enumerate(BLOCKS):
        if kind == 0:

            def put(at, value, delta=delta):
                value = (value * SCALE).astype(jnp.bfloat16)
                if delta == 0:
                    q[x, at, :] = value
                else:
                    qs[delta, at, :] = value
        else:

            def put(at, value, delta=delta, kind=kind):
                cols = pl.ds((kind - 1) * GW, GW)
                if delta == 0:
                    kv[SIDE + x, at, cols] = value.astype(jnp.bfloat16)
                else:
                    kvs[delta, at, cols] = value.astype(jnp.bfloat16)

        product(i, put)
        if delta == 0 and kind == 2:
            sent += up_down(0)
        if delta and kind == 2:
            across[delta] = pltpu.make_async_remote_copy(
                kvs.at[delta], kv.at[SIDE + x], xs.at[delta], xr.at[delta],
                device_id=device(y, x + delta), device_id_type=MESH,
            )
            across[delta].start()
        if delta and kind == 0:
            copy = pltpu.make_async_remote_copy(
                qs.at[delta], q.at[x], qss.at[delta], qsr.at[delta],
                device_id=device(y, x + delta), device_id_type=MESH,
            )
            copy.start()
            sent.append(copy)
    for delta in (1, 3, 2):
        across[delta].wait()
        sent += up_down(delta)
    for copy in sent:
        copy.wait()


def exchange(normed, w_qkv):
    dma = pltpu.SemaphoreType.DMA
    vmem = pl.BlockSpec(memory_space=pltpu.VMEM)
    return pl.pallas_call(
        exchange_kernel,
        out_shape=(
            jax.ShapeDtypeStruct((3 * SIDE, ROWS, 2 * GW), jnp.bfloat16),
            jax.ShapeDtypeStruct((SIDE, ROWS, GW), jnp.bfloat16),
        ),
        in_specs=[vmem, pl.BlockSpec(memory_space=pl.ANY)],
        out_specs=(vmem, vmem),
        scratch_shapes=[
            pltpu.VMEM((len(BLOCKS), D, GW), jnp.bfloat16),
            pltpu.VMEM((SIDE, ROWS, 2 * GW), jnp.bfloat16),
            pltpu.VMEM((SIDE, ROWS, GW), jnp.bfloat16),
            dma((len(BLOCKS),)),
            dma((SIDE,)),
            dma((SIDE,)),
            dma((SIDE,)),
            dma((SIDE,)),
            dma((2, SIDE)),
            dma((2, SIDE)),
        ],
        compiler_params=pltpu.CompilerParams(
            collective_id=0, has_side_effects=True, vmem_limit_bytes=VMEM
        ),
        name="exchange",
    )(normed, w_qkv)


def attend_kernel(counts, q, kv, out, keys, vals, masked, s0, s1, m0, m1, acc):
    low = lax.broadcasted_iota(jnp.int32, (1, 128), 1) < HEAD_DIM
    one = jnp.ones((BLK, 128), jnp.bfloat16)

    def pack(slot, at):
        frame, block = slot // MOSTB, slot % MOSTB
        live = block < counts[frame]

        @pl.when(live)
        def _():
            rows = pl.ds(pl.multiple_of(block * BLK, BLK), BLK)
            to = pl.ds(pl.multiple_of(at * BLK, BLK), BLK)
            for c in range(PAIRS):
                cols = slice(c * 128, (c + 1) * 128)
                keys[c, to, :] = kv[frame, rows, cols]
                v = kv[frame, rows, GW + c * 128 : GW + (c + 1) * 128]
                vals[c, 0, to, :] = jnp.where(low, v, one)
                vals[c, 1, to, :] = jnp.where(low, one, v)

        return at + live.astype(jnp.int32)

    total = lax.fori_loop(0, 3 * SIDE * MOSTB, pack, 0)
    tail = pl.ds(pl.multiple_of(total * BLK, BLK), CH)
    for c in range(PAIRS):
        keys[c, tail, :] = jnp.zeros((CH, 128), jnp.bfloat16)
        for h in range(2):
            vals[c, h, tail, :] = jnp.zeros((CH, 128), jnp.bfloat16)

    def frame_rows(f, first, blocks, rows):
        chunks = pl.cdiv(blocks, CH // BLK)
        limit = blocks * BLK
        for c in range(PAIRS):
            value = q[f, 0:rows, c * 128 : (c + 1) * 128]
            zero = jnp.zeros_like(value)
            masked[2 * c, 0:rows, :] = jnp.where(low, value, zero)
            masked[2 * c + 1, 0:rows, :] = jnp.where(low, zero, value)

        def score(head, j, s, m):
            at = pl.ds(pl.multiple_of(first * BLK + j * CH, BLK), CH)
            value = lax.dot_general(
                masked[head, 0:rows, :], keys[head // 2, at, :],
                (((1,), (1,)), ((), ())), preferred_element_type=jnp.float32,
            )
            col = lax.broadcasted_iota(jnp.int32, (1, CH), 1) + j * CH
            value = jnp.where(col < limit, value, -1e30)
            s[j, 0:rows, :] = value
            top = m[0:rows, :]
            for t in range(CH // 128):
                top = jnp.maximum(top, value[:, t * 128 : (t + 1) * 128])
            m[0:rows, :] = top

        def begin(m):
            m[0:rows, :] = jnp.full((rows, 128), -1e30, jnp.float32)

        def settle(m):
            m[0:rows, :] = jnp.broadcast_to(
                jnp.max(m[0:rows, :], axis=1, keepdims=True), (rows, 128)
            )

        def weigh(head, j, s, m):
            at = pl.ds(pl.multiple_of(first * BLK + j * CH, BLK), CH)
            top = m[0:rows, :]
            value = s[j, 0:rows, :]
            p = jnp.exp2(value - jnp.concatenate([top] * (CH // 128), axis=1)).astype(jnp.bfloat16)
            acc[0:rows, :] += jnp.dot(
                p, vals[head // 2, head % 2, at, :], preferred_element_type=jnp.float32
            )

        def finish(head):
            value = acc[0:rows, :]
            ratio = value / pltpu.roll(value, HEAD_DIM, 1)
            cols = slice((head // 2) * 128, (head // 2 + 1) * 128)
            if head % 2 == 0:
                out[f, 0:rows, cols] = ratio.astype(jnp.bfloat16)
            else:
                before = out[f, 0:rows, cols]
                out[f, 0:rows, cols] = jnp.where(low, before, ratio.astype(jnp.bfloat16))

        bufs = ((s0, m0), (s1, m1))
        begin(m0)
        lax.fori_loop(0, chunks, lambda j, t: (score(0, j, s0, m0), t)[1], 0)
        for head in range(2 * PAIRS):
            s, m = bufs[head % 2]
            sn, mn = bufs[(head + 1) % 2]
            settle(m)
            acc[0:rows, :] = jnp.zeros((rows, 128), jnp.float32)
            more = head + 1 < 2 * PAIRS
            if more:
                begin(mn)

            def step(j, t, head=head, s=s, m=m, sn=sn, mn=mn, more=more):
                if more:
                    score(head + 1, j, sn, mn)
                weigh(head, j, s, m)
                return t

            lax.fori_loop(0, chunks, step, 0)
            finish(head)

    def frame_body(f, first):
        blocks = counts[f]
        for k in range(1, 2 * SIDE + 1):
            blocks += counts[f + k]
        own = counts[SIDE + f]
        for n in range(1, MOSTB + 1):

            @pl.when(own == n)
            def _(n=n):
                frame_rows(f, first, blocks, n * BLK)
                if n < MOSTB:
                    out[f, n * BLK :, :] = jnp.zeros((ROWS - n * BLK, GW), jnp.bfloat16)

        return first + counts[f]

    lax.fori_loop(0, SIDE, frame_body, 0)


def attend(counts, q, kv):
    vmem = pl.BlockSpec(memory_space=pltpu.VMEM)
    return pl.pallas_call(
        attend_kernel,
        out_shape=jax.ShapeDtypeStruct((SIDE, ROWS, GW), jnp.bfloat16),
        in_specs=[pl.BlockSpec(memory_space=pltpu.SMEM), vmem, vmem],
        out_specs=vmem,
        scratch_shapes=[
            pltpu.VMEM((PAIRS, KROWS, 128), jnp.bfloat16),
            pltpu.VMEM((PAIRS, 2, KROWS, 128), jnp.bfloat16),
            pltpu.VMEM((2 * PAIRS, ROWS, 128), jnp.bfloat16),
            pltpu.VMEM((NCH, ROWS, CH), jnp.float32),
            pltpu.VMEM((NCH, ROWS, CH), jnp.float32),
            pltpu.VMEM((ROWS, 128), jnp.float32),
            pltpu.VMEM((ROWS, 128), jnp.float32),
            pltpu.VMEM((ROWS, 128), jnp.float32),
        ],
        compiler_params=pltpu.CompilerParams(vmem_limit_bytes=VMEM),
        name="attend",
    )(counts, q, kv)


def project_kernel(part, w, out, got, wbuf, total, wsem, ss, rs):
    y, x = place()
    order = (0, 1, 3, 2)
    loads = []
    for i, delta in enumerate(order):
        row = pl.multiple_of(((x - delta) % SIDE) * GW, GW)
        load = pltpu.make_async_copy(w.at[pl.ds(row, GW), :], wbuf.at[i], wsem.at[i])
        load.start()
        loads.append(load)
    barrier = pltpu.get_barrier_semaphore()
    for delta in (1, 2, 3):
        pl.semaphore_signal(barrier, inc=1, device_id=device(y, x + delta), device_id_type=MESH)
    pl.semaphore_wait(barrier, 3)
    copies = {}
    for delta in (2, 1, 3):
        copies[delta] = pltpu.make_async_remote_copy(
            part.at[(x + delta) % SIDE], got.at[delta], ss.at[delta], rs.at[delta],
            device_id=device(y, x + delta), device_id_type=MESH,
        )
        copies[delta].start()
    for i, delta in enumerate(order):
        loads[i].wait()
        if delta:
            copies[delta].wait()

        def rows(r, carry, i=i, delta=delta):
            at = pl.ds(pl.multiple_of(r * BLK, BLK), BLK)
            block = got[delta, at, :] if delta else part[x, at, :]
            value = jnp.dot(block, wbuf[i], preferred_element_type=jnp.float32)
            if i:
                value += total[at, :]
            if i < SIDE - 1:
                total[at, :] = value
            else:
                scale = lax.rsqrt(jnp.mean(value * value, axis=-1, keepdims=True) + 1e-06)
                out[at, :] = (value * scale).astype(jnp.bfloat16)
            return carry

        lax.fori_loop(0, MOSTB, rows, 0)


def project(part, w_out):
    dma = pltpu.SemaphoreType.DMA
    vmem = pl.BlockSpec(memory_space=pltpu.VMEM)
    return pl.pallas_call(
        project_kernel,
        out_shape=jax.ShapeDtypeStruct((ROWS, D), jnp.bfloat16),
        in_specs=[vmem, pl.BlockSpec(memory_space=pl.ANY)],
        out_specs=vmem,
        scratch_shapes=[
            pltpu.VMEM((SIDE, ROWS, GW), jnp.bfloat16),
            pltpu.VMEM((SIDE, GW, D), jnp.bfloat16),
            pltpu.VMEM((ROWS, D), jnp.float32),
            dma((SIDE,)),
            dma((SIDE,)),
            dma((SIDE,)),
        ],
        compiler_params=pltpu.CompilerParams(
            collective_id=1, has_side_effects=True, vmem_limit_bytes=VMEM
        ),
        name="project",
    )(part, w_out)


def scatter_kernel(order, count, block, out):
    live = pl.program_id(0) < count[0]

    @pl.when(live)
    def _():
        out[...] = block[...]

    @pl.when(jnp.logical_not(live))
    def _():
        out[...] = jnp.zeros_like(out)


def scatter(order_row, count, normalized):
    blocks = order_row.shape[0]
    return pl.pallas_call(
        scatter_kernel,
        grid_spec=pltpu.PrefetchScalarGridSpec(
            num_scalar_prefetch=2,
            grid=(blocks,),
            in_specs=[pl.BlockSpec((BLK, D), lambda j, order, count: (jnp.minimum(j, MOSTB - 1), 0))],
            out_specs=pl.BlockSpec((BLK, D), lambda j, order, count: (order[j], 0)),
        ),
        out_shape=jax.ShapeDtypeStruct((blocks * BLK, D), jnp.bfloat16),
        name="scatter",
    )(order_row, count, normalized)


def shards(tokens, keep_count, keep_order, w_qkv, w_out):
    here = lax.axis_index("frame")
    order_row = keep_order[0]
    own_count = lax.dynamic_slice(keep_count, (here,), (1,))
    row = here // SIDE
    around = lax.dynamic_slice(
        jnp.concatenate([keep_count, keep_count]), (((row + SIDE - 1) % SIDE) * SIDE,), (3 * SIDE,)
    )
    normed = norm_kept(order_row, tokens)
    kv, q = exchange(normed, w_qkv)
    part = attend(around, q, kv)
    normalized = project(part, w_out)
    return scatter(order_row, own_count, normalized)


def solution(mesh):
    return jax.shard_map(
        shards,
        mesh=mesh,
        in_specs=(P(("orbit", "frame"), None), P("orbit"), P(("orbit", "frame"), None), P(), P()),
        out_specs=P(("orbit", "frame"), None),
        check_vma=False,
    )
```

```python
import functools

import jax
import jax.numpy as jnp
from jax import lax
from jax.experimental import pallas as pl
from jax.experimental.pallas import tpu as pltpu
from jax.sharding import PartitionSpec as P

D = 1536
HEADS = 24
HEAD_DIM = 64
BLK = 128
MOSTB = 3
ROWS = MOSTB * BLK
SIDE = 4
GW = 384
PAIRS = 3
CH = 512
NCH = 7
KROWS = 36 * BLK + CH
SCALE = HEAD_DIM ** (-0.5) * 1.4426950408889634
VMEM = 60 * 2**20
MESH = pl.DeviceIdType.MESH


def place():
    me = lax.axis_index("frame")
    return me // SIDE, me % SIDE


def device(y, x):
    return {"frame": (y % SIDE) * SIDE + x % SIDE}


def norm_kernel(order, tok, out):
    wide = tok[...].astype(jnp.float32)
    scale = lax.rsqrt(jnp.mean(wide * wide, axis=-1, keepdims=True) + 1e-06)
    out[...] = (wide * scale).astype(jnp.bfloat16)


def norm_kept(order_row, tokens):
    return pl.pallas_call(
        norm_kernel,
        grid_spec=pltpu.PrefetchScalarGridSpec(
            num_scalar_prefetch=1,
            grid=(MOSTB,),
            in_specs=[pl.BlockSpec((BLK, D), lambda j, order: (order[0, j], 0))],
            out_specs=pl.BlockSpec((BLK, D), lambda j, order: (j, 0)),
        ),
        out_shape=jax.ShapeDtypeStruct((ROWS, D), jnp.bfloat16),
        name="norm_kept",
    )(order_row, tokens)


BLOCKS = ((0, 1), (0, 2), (1, 1), (1, 2), (3, 1), (3, 2), (2, 1), (2, 2), (1, 0), (3, 0), (2, 0), (0, 0))
FW = 256
LW = GW - FW


def exchange_kernel(
    normed, w, below, row, above, last, q, wbuf, kvs, lasts, qs,
    wsem, xs, xr, ls, lr, qss, qsr, ys, yr,
):
    y, x = place()
    loads = []
    for i, (delta, kind) in enumerate(BLOCKS):
        col = pl.multiple_of(kind * (HEADS * HEAD_DIM) + ((x + delta) % SIDE) * GW, 128)
        load = pltpu.make_async_copy(w.at[:, pl.ds(col, GW)], wbuf.at[i], wsem.at[i])
        load.start()
        loads.append(load)
    barrier = pltpu.get_barrier_semaphore()
    peers = [(0, 1), (0, 2), (0, 3), (1, 0), (3, 0)]
    for dy, dx in peers:
        pl.semaphore_signal(barrier, inc=1, device_id=device(y + dy, x + dx), device_id_type=MESH)
    pl.semaphore_wait(barrier, len(peers))

    def product(i, put):
        loads[i].wait()

        def rows(r, carry):
            at = pl.ds(pl.multiple_of(r * BLK, BLK), BLK)
            value = jnp.dot(normed[at, :], wbuf[i], preferred_element_type=jnp.float32)
            put(at, value)
            return carry

        lax.fori_loop(0, MOSTB, rows, 0)

    def across(src, dst, send, recv, delta):
        return pltpu.make_async_remote_copy(
            src.at[delta], dst.at[delta], send.at[delta], recv.at[delta],
            device_id=device(y, x + delta), device_id_type=MESH,
        )

    first = {delta: across(kvs, row, xs, xr, delta) for delta in (1, 2, 3)}
    later = {delta: across(lasts, last, ls, lr, delta) for delta in (1, 2, 3)}
    query = {delta: across(qs, q, qss, qsr, delta) for delta in (1, 2, 3)}
    sent = []

    def up_down(delta):
        for way, (dy, to) in enumerate(((1, below), (-1, above))):
            copy = pltpu.make_async_remote_copy(
                row.at[delta], to.at[delta], ys.at[way, delta], yr.at[way, delta],
                device_id=device(y + dy, x), device_id_type=MESH,
            )
            copy.start()
            sent.append(copy)

    for i, (delta, kind) in enumerate(BLOCKS):
        if kind == 0:
            to = q if delta == 0 else qs

            def put(at, value, delta=delta, to=to):
                to[delta, at, :] = (value * SCALE).astype(jnp.bfloat16)
        else:
            to, rest = (row, last) if delta == 0 else (kvs, lasts)

            def put(at, value, delta=delta, kind=kind, to=to, rest=rest):
                value = value.astype(jnp.bfloat16)
                to[delta, at, pl.ds((kind - 1) * FW, FW)] = value[:, :FW]
                rest[delta, at, pl.ds((kind - 1) * LW, LW)] = value[:, FW:]

        product(i, put)
        if kind == 2:
            if delta == 0:
                up_down(0)
            elif delta != 2:
                first[delta].start()
    first[1].wait()
    up_down(1)
    first[2].start()
    first[3].wait()
    up_down(3)
    for delta in (1, 3, 2):
        query[delta].start()
    first[2].wait()
    up_down(2)
    for delta in (1, 3, 2):
        later[delta].start()
    for copy in [*query.values(), *later.values(), *sent]:
        copy.wait()


def exchange(normed, w_qkv):
    dma = pltpu.SemaphoreType.DMA
    vmem = pl.BlockSpec(memory_space=pltpu.VMEM)
    shapes = [(SIDE, ROWS, 2 * FW)] * 3 + [(SIDE, ROWS, 2 * LW), (SIDE, ROWS, GW)]
    return pl.pallas_call(
        exchange_kernel,
        out_shape=[jax.ShapeDtypeStruct(shape, jnp.bfloat16) for shape in shapes],
        in_specs=[vmem, pl.BlockSpec(memory_space=pl.ANY)],
        out_specs=[vmem] * 5,
        scratch_shapes=[
            pltpu.VMEM((len(BLOCKS), D, GW), jnp.bfloat16),
            pltpu.VMEM((SIDE, ROWS, 2 * FW), jnp.bfloat16),
            pltpu.VMEM((SIDE, ROWS, 2 * LW), jnp.bfloat16),
            pltpu.VMEM((SIDE, ROWS, GW), jnp.bfloat16),
            dma((len(BLOCKS),)),
            *[dma((SIDE,))] * 6,
            dma((2, SIDE)),
            dma((2, SIDE)),
        ],
        compiler_params=pltpu.CompilerParams(
            collective_id=0, has_side_effects=True, vmem_limit_bytes=34 * 2**20
        ),
        name="exchange",
    )(normed, w_qkv)


def attend_kernel(start, pairs, keep, q, below, row, above, out, live, keys, vals, masked, s0, s1, m0, m1, acc):
    y, x = place()
    for k in range(3 * SIDE):
        live[k] = keep[((y + SIDE - 1) * SIDE + k) % (SIDE * SIDE)]
    low = lax.broadcasted_iota(jnp.int32, (1, 128), 1) < HEAD_DIM
    one = jnp.ones((BLK, 128), jnp.bfloat16)
    counts = live
    total = 0
    for k, kv in enumerate((below, row, above)):

        def pack(slot, at, k=k, kv=kv):
            frame, block = slot // MOSTB, slot % MOSTB
            back = (x + SIDE - frame) % SIDE
            used = block < counts[k * SIDE + frame]

            @pl.when(used)
            def _():
                rows = pl.ds(pl.multiple_of(block * BLK, BLK), BLK)
                to = pl.ds(pl.multiple_of(at * BLK, BLK), BLK)
                for c in range(pairs):
                    keys[c, to, :] = kv[back, rows, c * 128 : (c + 1) * 128]
                    v = kv[back, rows, (pairs + c) * 128 : (pairs + c + 1) * 128]
                    vals[c, 0, to, :] = jnp.where(low, v, one)
                    vals[c, 1, to, :] = jnp.where(low, one, v)

            return at + used.astype(jnp.int32)

        total = lax.fori_loop(0, SIDE * MOSTB, pack, total)
    tail = pl.ds(pl.multiple_of(total * BLK, BLK), CH)
    for c in range(pairs):
        keys[c, tail, :] = jnp.zeros((CH, 128), jnp.bfloat16)
        for h in range(2):
            vals[c, h, tail, :] = jnp.zeros((CH, 128), jnp.bfloat16)

    def frame_rows(d, first, blocks, rows):
        chunks = pl.cdiv(blocks, CH // BLK)
        limit = blocks * BLK
        for c in range(pairs):
            value = q[d, 0:rows, (start + c) * 128 : (start + c + 1) * 128]
            zero = jnp.zeros_like(value)
            masked[2 * c, 0:rows, :] = jnp.where(low, value, zero)
            masked[2 * c + 1, 0:rows, :] = jnp.where(low, zero, value)

        def score(head, j, s, m):
            at = pl.ds(pl.multiple_of(first * BLK + j * CH, BLK), CH)
            value = lax.dot_general(
                masked[head, 0:rows, :], keys[head // 2, at, :],
                (((1,), (1,)), ((), ())), preferred_element_type=jnp.float32,
            )
            col = lax.broadcasted_iota(jnp.int32, (1, CH), 1) + j * CH
            value = jnp.where(col < limit, value, -1e30)
            s[j, 0:rows, :] = value
            top = m[0:rows, :]
            for t in range(CH // 128):
                top = jnp.maximum(top, value[:, t * 128 : (t + 1) * 128])
            m[0:rows, :] = top

        def begin(m):
            m[0:rows, :] = jnp.full((rows, 128), -1e30, jnp.float32)

        def settle(m):
            m[0:rows, :] = jnp.broadcast_to(
                jnp.max(m[0:rows, :], axis=1, keepdims=True), (rows, 128)
            )

        def weigh(head, j, s, m):
            at = pl.ds(pl.multiple_of(first * BLK + j * CH, BLK), CH)
            top = m[0:rows, :]
            value = s[j, 0:rows, :]
            p = jnp.exp2(value - jnp.concatenate([top] * (CH // 128), axis=1)).astype(jnp.bfloat16)
            acc[0:rows, :] += jnp.dot(
                p, vals[head // 2, head % 2, at, :], preferred_element_type=jnp.float32
            )

        def finish(head):
            value = acc[0:rows, :]
            ratio = value / pltpu.roll(value, HEAD_DIM, 1)
            cols = slice((head // 2) * 128, (head // 2 + 1) * 128)
            if head % 2 == 0:
                out[d, 0:rows, cols] = ratio.astype(jnp.bfloat16)
            else:
                before = out[d, 0:rows, cols]
                out[d, 0:rows, cols] = jnp.where(low, before, ratio.astype(jnp.bfloat16))

        bufs = ((s0, m0), (s1, m1))
        begin(m0)
        lax.fori_loop(0, chunks, lambda j, t: (score(0, j, s0, m0), t)[1], 0)
        for head in range(2 * pairs):
            s, m = bufs[head % 2]
            sn, mn = bufs[(head + 1) % 2]
            settle(m)
            acc[0:rows, :] = jnp.zeros((rows, 128), jnp.float32)
            more = head + 1 < 2 * pairs
            if more:
                begin(mn)

            def step(j, t, head=head, s=s, m=m, sn=sn, mn=mn, more=more):
                if more:
                    score(head + 1, j, sn, mn)
                weigh(head, j, s, m)
                return t

            lax.fori_loop(0, chunks, step, 0)
            finish(head)

    def frame_body(f, first):
        blocks = counts[f]
        for k in range(1, 2 * SIDE + 1):
            blocks += counts[f + k]
        own = counts[SIDE + f]
        d = (x + SIDE - f) % SIDE
        for n in range(1, MOSTB + 1):

            @pl.when(own == n)
            def _(n=n):
                frame_rows(d, first, blocks, n * BLK)
                if n < MOSTB:
                    out[d, n * BLK :, :] = jnp.zeros((ROWS - n * BLK, pairs * 128), jnp.bfloat16)

        return first + counts[f]

    lax.fori_loop(0, SIDE, frame_body, 0)


def attend(start, pairs, keep_count, q, below, row, above):
    vmem = pl.BlockSpec(memory_space=pltpu.VMEM)
    return pl.pallas_call(
        functools.partial(attend_kernel, start, pairs),
        out_shape=jax.ShapeDtypeStruct((SIDE, ROWS, pairs * 128), jnp.bfloat16),
        in_specs=[pl.BlockSpec(memory_space=pltpu.SMEM)] + [vmem] * 4,
        out_specs=vmem,
        scratch_shapes=[
            pltpu.SMEM((3 * SIDE,), jnp.int32),
            pltpu.VMEM((pairs, KROWS, 128), jnp.bfloat16),
            pltpu.VMEM((pairs, 2, KROWS, 128), jnp.bfloat16),
            pltpu.VMEM((2 * pairs, ROWS, 128), jnp.bfloat16),
            pltpu.VMEM((NCH, ROWS, CH), jnp.float32),
            pltpu.VMEM((NCH, ROWS, CH), jnp.float32),
            pltpu.VMEM((ROWS, 128), jnp.float32),
            pltpu.VMEM((ROWS, 128), jnp.float32),
            pltpu.VMEM((ROWS, 128), jnp.float32),
        ],
        compiler_params=pltpu.CompilerParams(vmem_limit_bytes=VMEM // 2),
        cost_estimate=pl.CostEstimate(
            flops=pairs * 18 * 10**9, bytes_accessed=pairs * 2**21, transcendentals=0
        ),
        name="attend",
    )(keep_count, q, below, row, above)


def project_kernel(part, rest, w, out, got, wbuf, total, wsem, ss, rs, ts, tr):
    y, x = place()
    order = (0, 1, 3, 2)
    loads = []
    for i, delta in enumerate(order):
        row = pl.multiple_of(((x - delta) % SIDE) * GW, GW)
        load = pltpu.make_async_copy(w.at[pl.ds(row, GW), :], wbuf.at[i], wsem.at[i])
        load.start()
        loads.append(load)
    barrier = pltpu.get_barrier_semaphore()
    for delta in (1, 2, 3):
        pl.semaphore_signal(barrier, inc=1, device_id=device(y, x + delta), device_id_type=MESH)
    pl.semaphore_wait(barrier, 3)
    copies = {}
    for delta in (2, 1, 3):
        copies[delta] = [
            pltpu.make_async_remote_copy(
                src.at[(SIDE - delta) % SIDE], got.at[delta, :, cols], send.at[delta], recv.at[delta],
                device_id=device(y, x + delta), device_id_type=MESH,
            )
            for src, cols, send, recv in (
                (part, pl.ds(0, FW), ss, rs),
                (rest, pl.ds(FW, LW), ts, tr),
            )
        ]
        for copy in copies[delta]:
            copy.start()
    got[0, :, :FW] = part[0]
    got[0, :, FW:] = rest[0]
    for i, delta in enumerate(order):
        loads[i].wait()
        if delta:
            for copy in copies[delta]:
                copy.wait()

        def rows(r, carry, i=i, delta=delta):
            at = pl.ds(pl.multiple_of(r * BLK, BLK), BLK)
            value = jnp.dot(got[delta, at, :], wbuf[i], preferred_element_type=jnp.float32)
            if i:
                value += total[at, :]
            if i < SIDE - 1:
                total[at, :] = value
            else:
                scale = lax.rsqrt(jnp.mean(value * value, axis=-1, keepdims=True) + 1e-06)
                out[at, :] = (value * scale).astype(jnp.bfloat16)
            return carry

        lax.fori_loop(0, MOSTB, rows, 0)


def project(part, rest, w_out):
    dma = pltpu.SemaphoreType.DMA
    vmem = pl.BlockSpec(memory_space=pltpu.VMEM)
    return pl.pallas_call(
        project_kernel,
        out_shape=jax.ShapeDtypeStruct((ROWS, D), jnp.bfloat16),
        in_specs=[vmem, vmem, pl.BlockSpec(memory_space=pl.ANY)],
        out_specs=vmem,
        scratch_shapes=[
            pltpu.VMEM((SIDE, ROWS, GW), jnp.bfloat16),
            pltpu.VMEM((SIDE, GW, D), jnp.bfloat16),
            pltpu.VMEM((ROWS, D), jnp.float32),
            *[dma((SIDE,))] * 5,
        ],
        compiler_params=pltpu.CompilerParams(
            collective_id=1, has_side_effects=True, vmem_limit_bytes=24 * 2**20
        ),
        name="project",
    )(part, rest, w_out)


def scatter_kernel(order, count, block, out):
    live = pl.program_id(0) < count[lax.axis_index("frame")]

    @pl.when(live)
    def _():
        out[...] = block[...]

    @pl.when(jnp.logical_not(live))
    def _():
        out[...] = jnp.zeros_like(out)


def scatter(order_row, count, normalized):
    blocks = order_row.shape[1]
    return pl.pallas_call(
        scatter_kernel,
        grid_spec=pltpu.PrefetchScalarGridSpec(
            num_scalar_prefetch=2,
            grid=(blocks,),
            in_specs=[pl.BlockSpec((BLK, D), lambda j, order, count: (jnp.minimum(j, MOSTB - 1), 0))],
            out_specs=pl.BlockSpec((BLK, D), lambda j, order, count: (order[0, j], 0)),
        ),
        out_shape=jax.ShapeDtypeStruct((blocks * BLK, D), jnp.bfloat16),
        name="scatter",
    )(order_row, count, normalized)


def shifted(value, steps):
    count = SIDE * SIDE
    return lax.ppermute(value, "frame", [(f, (f + steps) % count) for f in range(count)])


def shards(tokens, keep_count, keep_order, w_qkv, w_out):
    normed = norm_kept(keep_order, tokens)
    below, row, above, last, q = exchange(normed, w_qkv)
    last_below = shifted(last, SIDE)
    last_above = shifted(last, -SIDE)
    part = attend(0, 2, keep_count, q, below, row, above)
    rest = attend(2, 1, keep_count, q, last_below, last, last_above)
    normalized = project(part, rest, w_out)
    return scatter(keep_order, keep_count, normalized)


def solution(mesh):
    return jax.shard_map(
        shards,
        mesh=mesh,
        in_specs=(P(("orbit", "frame"), None), P("orbit"), P(("orbit", "frame"), None), P(), P()),
        out_specs=P(("orbit", "frame"), None),
        check_vma=False,
    )
```

```python
import functools

import jax
import jax.numpy as jnp
from jax import lax
from jax.experimental import pallas as pl
from jax.experimental.pallas import tpu as pltpu
from jax.sharding import PartitionSpec as P

D = 1536
HEADS = 24
HEAD_DIM = 64
BLK = 128
MOSTB = 3
ROWS = MOSTB * BLK
SIDE = 4
GW = 384
CH = 1024
WINDOW = 28 * BLK
KROWS = 36 * BLK + CH
SCALE = HEAD_DIM ** (-0.5) * 1.4426950408889634
MESH = pl.DeviceIdType.MESH


def place():
    me = lax.axis_index("frame")
    return me // SIDE, me % SIDE


def device(y, x):
    return {"frame": (y % SIDE) * SIDE + x % SIDE}


def norm_kernel(order, tok, out):
    wide = tok[...].astype(jnp.float32)
    scale = lax.rsqrt(jnp.mean(wide * wide, axis=-1, keepdims=True) + 1e-06)
    out[...] = (wide * scale).astype(jnp.bfloat16)


def norm_kept(order_row, tokens):
    return pl.pallas_call(
        norm_kernel,
        grid_spec=pltpu.PrefetchScalarGridSpec(
            num_scalar_prefetch=1,
            grid=(MOSTB,),
            in_specs=[pl.BlockSpec((BLK, D), lambda j, order: (order[0, j], 0))],
            out_specs=pl.BlockSpec((BLK, D), lambda j, order: (j, 0)),
        ),
        out_shape=jax.ShapeDtypeStruct((ROWS, D), jnp.bfloat16),
        name="norm_kept",
    )(order_row, tokens)


BLOCKS = ((0, 1), (0, 2), (1, 1), (1, 2), (3, 1), (3, 2), (2, 1), (2, 2), (1, 0), (3, 0), (2, 0), (0, 0))
FW = 256
LW = GW - FW


def exchange_kernel(
    normed, w, below, row, above, last, q, wbuf, kvs, lasts, qs,
    wsem, xs, xr, ls, lr, qss, qsr, ys, yr,
):
    y, x = place()
    loads = []
    for i, (delta, kind) in enumerate(BLOCKS):
        col = pl.multiple_of(kind * (HEADS * HEAD_DIM) + ((x + delta) % SIDE) * GW, 128)
        load = pltpu.make_async_copy(w.at[:, pl.ds(col, GW)], wbuf.at[i], wsem.at[i])
        load.start()
        loads.append(load)
    barrier = pltpu.get_barrier_semaphore()
    peers = [(0, 1), (0, 2), (0, 3), (1, 0), (3, 0)]
    for dy, dx in peers:
        pl.semaphore_signal(barrier, inc=1, device_id=device(y + dy, x + dx), device_id_type=MESH)
    pl.semaphore_wait(barrier, len(peers))

    def product(i, put):
        loads[i].wait()

        def rows(r, carry):
            at = pl.ds(pl.multiple_of(r * BLK, BLK), BLK)
            value = jnp.dot(normed[at, :], wbuf[i], preferred_element_type=jnp.float32)
            put(at, value)
            return carry

        lax.fori_loop(0, MOSTB, rows, 0)

    def across(src, dst, send, recv, delta):
        return pltpu.make_async_remote_copy(
            src.at[delta], dst.at[delta], send.at[delta], recv.at[delta],
            device_id=device(y, x + delta), device_id_type=MESH,
        )

    first = {delta: across(kvs, row, xs, xr, delta) for delta in (1, 2, 3)}
    later = {delta: across(lasts, last, ls, lr, delta) for delta in (1, 2, 3)}
    query = {delta: across(qs, q, qss, qsr, delta) for delta in (1, 2, 3)}
    sent = []

    def up_down(delta):
        for way, (dy, to) in enumerate(((1, below), (-1, above))):
            copy = pltpu.make_async_remote_copy(
                row.at[delta], to.at[delta], ys.at[way, delta], yr.at[way, delta],
                device_id=device(y + dy, x), device_id_type=MESH,
            )
            copy.start()
            sent.append(copy)

    for i, (delta, kind) in enumerate(BLOCKS):
        if kind == 0:
            to = q if delta == 0 else qs

            def put(at, value, delta=delta, to=to):
                to[delta, at, :] = (value * SCALE).astype(jnp.bfloat16)
        else:
            to, rest = (row, last) if delta == 0 else (kvs, lasts)

            def put(at, value, delta=delta, kind=kind, to=to, rest=rest):
                value = value.astype(jnp.bfloat16)
                to[delta, at, pl.ds((kind - 1) * FW, FW)] = value[:, :FW]
                rest[delta, at, pl.ds((kind - 1) * LW, LW)] = value[:, FW:]

        product(i, put)
        if kind == 2:
            if delta == 0:
                up_down(0)
            elif delta != 2:
                first[delta].start()
    first[1].wait()
    up_down(1)
    first[2].start()
    first[3].wait()
    up_down(3)
    for delta in (1, 3, 2):
        query[delta].start()
    first[2].wait()
    up_down(2)
    for delta in (1, 3, 2):
        later[delta].start()
    for copy in [*query.values(), *later.values(), *sent]:
        copy.wait()


def exchange(normed, w_qkv):
    dma = pltpu.SemaphoreType.DMA
    vmem = pl.BlockSpec(memory_space=pltpu.VMEM)
    shapes = [(SIDE, ROWS, 2 * FW)] * 3 + [(SIDE, ROWS, 2 * LW), (SIDE, ROWS, GW)]
    return pl.pallas_call(
        exchange_kernel,
        out_shape=[jax.ShapeDtypeStruct(shape, jnp.bfloat16) for shape in shapes],
        in_specs=[vmem, pl.BlockSpec(memory_space=pl.ANY)],
        out_specs=[vmem] * 5,
        scratch_shapes=[
            pltpu.VMEM((len(BLOCKS), D, GW), jnp.bfloat16),
            pltpu.VMEM((SIDE, ROWS, 2 * FW), jnp.bfloat16),
            pltpu.VMEM((SIDE, ROWS, 2 * LW), jnp.bfloat16),
            pltpu.VMEM((SIDE, ROWS, GW), jnp.bfloat16),
            dma((len(BLOCKS),)),
            *[dma((SIDE,))] * 6,
            dma((2, SIDE)),
            dma((2, SIDE)),
        ],
        compiler_params=pltpu.CompilerParams(
            collective_id=0, has_side_effects=True, vmem_limit_bytes=34 * 2**20
        ),
        name="exchange",
    )(normed, w_qkv)


def attend_kernel(start, pairs, keep, q, below, row, above, out, live, keys, vals, masked, s0, s1, m0, m1, acc):
    y, x = place()
    for k in range(3 * SIDE):
        live[k] = keep[((y + SIDE - 1) * SIDE + k) % (SIDE * SIDE)]
    low = lax.broadcasted_iota(jnp.int32, (1, 128), 1) < HEAD_DIM
    one = jnp.ones((BLK, 128), jnp.bfloat16)
    counts = live
    total = 0
    for k, kv in enumerate((below, row, above)):

        def pack(slot, at, k=k, kv=kv):
            frame, block = slot // MOSTB, slot % MOSTB
            back = (x + SIDE - frame) % SIDE
            used = block < counts[k * SIDE + frame]

            @pl.when(used)
            def _():
                rows = pl.ds(pl.multiple_of(block * BLK, BLK), BLK)
                to = pl.ds(pl.multiple_of(at * BLK, BLK), BLK)
                for c in range(pairs):
                    keys[c, to, :] = kv[back, rows, c * 128 : (c + 1) * 128]
                    v = kv[back, rows, (pairs + c) * 128 : (pairs + c + 1) * 128]
                    vals[c, 0, to, :] = jnp.where(low, v, one)
                    vals[c, 1, to, :] = jnp.where(low, one, v)

            return at + used.astype(jnp.int32)

        total = lax.fori_loop(0, SIDE * MOSTB, pack, total)
    tail = pl.ds(pl.multiple_of(total * BLK, BLK), CH)
    for c in range(pairs):
        keys[c, tail, :] = jnp.zeros((CH, 128), jnp.bfloat16)
        for h in range(2):
            vals[c, h, tail, :] = jnp.zeros((CH, 128), jnp.bfloat16)

    def frame_rows(d, first, blocks, rows):
        full, left = blocks // (CH // BLK), blocks % (CH // BLK)
        for c in range(pairs):
            value = q[d, 0:rows, (start + c) * 128 : (start + c + 1) * 128]
            zero = jnp.zeros_like(value)
            masked[2 * c, 0:rows, :] = jnp.where(low, value, zero)
            masked[2 * c + 1, 0:rows, :] = jnp.where(low, zero, value)

        def span(j, width):
            return (
                pl.ds(pl.multiple_of(first * BLK + j * CH, BLK), width),
                pl.ds(pl.multiple_of(j * CH, BLK), width),
            )

        def score(c, j, width, partial, s, m):
            at, cols = span(j, width)
            for h in range(2):
                value = lax.dot_general(
                    masked[2 * c + h, 0:rows, :], keys[c, at, :],
                    (((1,), (1,)), ((), ())), preferred_element_type=jnp.float32,
                )
                if partial:
                    col = lax.broadcasted_iota(jnp.int32, (1, width), 1)
                    value = jnp.where(col < left * BLK, value, -1e30)
                s[h, 0:rows, cols] = value
                top = m[h, 0:rows, :]
                for t in range(width // 128):
                    top = jnp.maximum(top, value[:, t * 128 : (t + 1) * 128])
                m[h, 0:rows, :] = top

        def weigh(c, j, width, s, m):
            at, cols = span(j, width)
            for h in range(2):
                top = jnp.concatenate([m[h, 0:rows, :]] * (width // 128), axis=1)
                p = jnp.exp2(s[h, 0:rows, cols] - top).astype(jnp.bfloat16)
                acc[h, 0:rows, :] += jnp.dot(p, vals[c, h, at, :], preferred_element_type=jnp.float32)

        bufs = ((s0, m0), (s1, m1))
        for stage in range(pairs + 1):
            s, m = bufs[(stage + 1) % 2]
            sn, mn = bufs[stage % 2]
            if stage:
                m[:, 0:rows, :] = jnp.broadcast_to(
                    jnp.max(m[:, 0:rows, :], axis=2, keepdims=True), (2, rows, 128)
                )
                acc[:, 0:rows, :] = jnp.zeros((2, rows, 128), jnp.float32)
            if stage < pairs:
                mn[:, 0:rows, :] = jnp.full((2, rows, 128), -1e30, jnp.float32)

            def step(j, width, partial, stage=stage, s=s, m=m, sn=sn, mn=mn):
                if stage < pairs:
                    score(stage, j, width, partial, sn, mn)
                if stage:
                    weigh(stage - 1, j, width, s, m)

            lax.fori_loop(0, full, lambda j, t, step=step: (step(j, CH, False), t)[1], 0)

            @pl.when((left > 0) & (left <= CH // BLK // 2))
            def _(step=step):
                step(full, CH // 2, True)

            @pl.when(left > CH // BLK // 2)
            def _(step=step):
                step(full, CH, True)

            if stage:
                even, odd = acc[0, 0:rows, :], acc[1, 0:rows, :]
                even = even / pltpu.roll(even, HEAD_DIM, 1)
                odd = odd / pltpu.roll(odd, HEAD_DIM, 1)
                out[d, 0:rows, (stage - 1) * 128 : stage * 128] = jnp.where(low, even, odd).astype(jnp.bfloat16)

    def frame_body(f, first):
        blocks = counts[f]
        for k in range(1, 2 * SIDE + 1):
            blocks += counts[f + k]
        own = counts[SIDE + f]
        d = (x + SIDE - f) % SIDE
        for n in range(1, MOSTB + 1):

            @pl.when(own == n)
            def _(n=n):
                frame_rows(d, first, blocks, n * BLK)
                if n < MOSTB:
                    out[d, n * BLK :, :] = jnp.zeros((ROWS - n * BLK, pairs * 128), jnp.bfloat16)

        return first + counts[f]

    lax.fori_loop(0, SIDE, frame_body, 0)


def attend(start, pairs, keep_count, q, below, row, above):
    vmem = pl.BlockSpec(memory_space=pltpu.VMEM)
    return pl.pallas_call(
        functools.partial(attend_kernel, start, pairs),
        out_shape=jax.ShapeDtypeStruct((SIDE, ROWS, pairs * 128), jnp.bfloat16),
        in_specs=[pl.BlockSpec(memory_space=pltpu.SMEM)] + [vmem] * 4,
        out_specs=vmem,
        scratch_shapes=[
            pltpu.SMEM((3 * SIDE,), jnp.int32),
            pltpu.VMEM((pairs, KROWS, 128), jnp.bfloat16),
            pltpu.VMEM((pairs, 2, KROWS, 128), jnp.bfloat16),
            pltpu.VMEM((2 * pairs, ROWS, 128), jnp.bfloat16),
            pltpu.VMEM((2, ROWS, WINDOW), jnp.float32),
            pltpu.VMEM((2, ROWS, WINDOW), jnp.float32),
            *[pltpu.VMEM((2, ROWS, 128), jnp.float32)] * 3,
        ],
        compiler_params=pltpu.CompilerParams(vmem_limit_bytes=42 * 2**20),
        cost_estimate=pl.CostEstimate(
            flops=pairs * 18 * 10**9, bytes_accessed=pairs * 2**21, transcendentals=0
        ),
        name="attend",
    )(keep_count, q, below, row, above)


def project_kernel(part, rest, w, out, got, wbuf, total, wsem, ss, rs, ts, tr):
    y, x = place()
    order = (0, 1, 3, 2)
    loads = []
    for i, delta in enumerate(order):
        row = pl.multiple_of(((x - delta) % SIDE) * GW, GW)
        load = pltpu.make_async_copy(w.at[pl.ds(row, GW), :], wbuf.at[i], wsem.at[i])
        load.start()
        loads.append(load)
    barrier = pltpu.get_barrier_semaphore()
    for delta in (1, 2, 3):
        pl.semaphore_signal(barrier, inc=1, device_id=device(y, x + delta), device_id_type=MESH)
    pl.semaphore_wait(barrier, 3)
    copies = {}
    for delta in (2, 1, 3):
        copies[delta] = [
            pltpu.make_async_remote_copy(
                src.at[(SIDE - delta) % SIDE], got.at[delta, :, cols], send.at[delta], recv.at[delta],
                device_id=device(y, x + delta), device_id_type=MESH,
            )
            for src, cols, send, recv in (
                (part, pl.ds(0, FW), ss, rs),
                (rest, pl.ds(FW, LW), ts, tr),
            )
        ]
        for copy in copies[delta]:
            copy.start()
    got[0, :, :FW] = part[0]
    got[0, :, FW:] = rest[0]
    for i, delta in enumerate(order):
        loads[i].wait()
        if delta:
            for copy in copies[delta]:
                copy.wait()

        def rows(r, carry, i=i, delta=delta):
            at = pl.ds(pl.multiple_of(r * BLK, BLK), BLK)
            value = jnp.dot(got[delta, at, :], wbuf[i], preferred_element_type=jnp.float32)
            if i:
                value += total[at, :]
            if i < SIDE - 1:
                total[at, :] = value
            else:
                scale = lax.rsqrt(jnp.mean(value * value, axis=-1, keepdims=True) + 1e-06)
                out[at, :] = (value * scale).astype(jnp.bfloat16)
            return carry

        lax.fori_loop(0, MOSTB, rows, 0)


def project(part, rest, w_out):
    dma = pltpu.SemaphoreType.DMA
    vmem = pl.BlockSpec(memory_space=pltpu.VMEM)
    return pl.pallas_call(
        project_kernel,
        out_shape=jax.ShapeDtypeStruct((ROWS, D), jnp.bfloat16),
        in_specs=[vmem, vmem, pl.BlockSpec(memory_space=pl.ANY)],
        out_specs=vmem,
        scratch_shapes=[
            pltpu.VMEM((SIDE, ROWS, GW), jnp.bfloat16),
            pltpu.VMEM((SIDE, GW, D), jnp.bfloat16),
            pltpu.VMEM((ROWS, D), jnp.float32),
            *[dma((SIDE,))] * 5,
        ],
        compiler_params=pltpu.CompilerParams(
            collective_id=1, has_side_effects=True, vmem_limit_bytes=24 * 2**20
        ),
        name="project",
    )(part, rest, w_out)


def scatter_kernel(order, count, block, out):
    live = pl.program_id(0) < count[lax.axis_index("frame")]

    @pl.when(live)
    def _():
        out[...] = block[...]

    @pl.when(jnp.logical_not(live))
    def _():
        out[...] = jnp.zeros_like(out)


def scatter(order_row, count, normalized):
    blocks = order_row.shape[1]
    return pl.pallas_call(
        scatter_kernel,
        grid_spec=pltpu.PrefetchScalarGridSpec(
            num_scalar_prefetch=2,
            grid=(blocks,),
            in_specs=[pl.BlockSpec((BLK, D), lambda j, order, count: (jnp.minimum(j, MOSTB - 1), 0))],
            out_specs=pl.BlockSpec((BLK, D), lambda j, order, count: (order[0, j], 0)),
        ),
        out_shape=jax.ShapeDtypeStruct((blocks * BLK, D), jnp.bfloat16),
        name="scatter",
    )(order_row, count, normalized)


def shifted(value, steps):
    count = SIDE * SIDE
    return lax.ppermute(value, "frame", [(f, (f + steps) % count) for f in range(count)])


def shards(tokens, keep_count, keep_order, w_qkv, w_out):
    normed = norm_kept(keep_order, tokens)
    below, row, above, last, q = exchange(normed, w_qkv)
    last_below = shifted(last, SIDE)
    last_above = shifted(last, -SIDE)
    part = attend(0, 2, keep_count, q, below, row, above)
    rest = attend(2, 1, keep_count, q, last_below, last, last_above)
    normalized = project(part, rest, w_out)
    return scatter(keep_order, keep_count, normalized)


def solution(mesh):
    return jax.shard_map(
        shards,
        mesh=mesh,
        in_specs=(P(("orbit", "frame"), None), P("orbit"), P(("orbit", "frame"), None), P(), P()),
        out_specs=P(("orbit", "frame"), None),
        check_vma=False,
    )
```

```python
import functools

import jax
import jax.numpy as jnp
from jax import lax
from jax.experimental import pallas as pl
from jax.experimental.pallas import tpu as pltpu
from jax.sharding import PartitionSpec as P

D = 1536
HEADS = 24
HEAD_DIM = 64
BLK = 128
MOSTB = 3
ROWS = MOSTB * BLK
SIDE = 4
GW = 384
CH = 1024
WINDOW = 28 * BLK
KROWS = 36 * BLK + CH
SCALE = HEAD_DIM ** (-0.5) * 1.4426950408889634
MESH = pl.DeviceIdType.MESH


def place():
    me = lax.axis_index("frame")
    return me // SIDE, me % SIDE


def device(y, x):
    return {"frame": (y % SIDE) * SIDE + x % SIDE}


def norm_kernel(order, tokens, out, kept, sems):
    loads = []
    for j in range(MOSTB):
        rows = pl.ds(pl.multiple_of(order[0, j] * BLK, BLK), BLK)
        loads.append(pltpu.make_async_copy(tokens.at[rows, :], kept.at[j], sems.at[j]))
        loads[j].start()
    for j in range(MOSTB):
        loads[j].wait()
        wide = kept[j].astype(jnp.float32)
        scale = lax.rsqrt(jnp.mean(wide * wide, axis=-1, keepdims=True) + 1e-06)
        out[j * BLK : (j + 1) * BLK, :] = (wide * scale).astype(jnp.bfloat16)


def norm_kept(keep_order, tokens):
    return pl.pallas_call(
        norm_kernel,
        in_specs=[pl.BlockSpec(memory_space=pltpu.SMEM), pl.BlockSpec(memory_space=pltpu.HBM)],
        out_specs=pl.BlockSpec(memory_space=pltpu.VMEM),
        out_shape=jax.ShapeDtypeStruct((ROWS, D), jnp.bfloat16),
        scratch_shapes=[pltpu.VMEM((MOSTB, BLK, D), jnp.bfloat16), pltpu.SemaphoreType.DMA((MOSTB,))],
        compiler_params=pltpu.CompilerParams(vmem_limit_bytes=12 * 2**20),
        name="norm_kept",
    )(keep_order, tokens)


BLOCKS = ((1, 1), (1, 2), (0, 1), (0, 2), (3, 1), (3, 2), (2, 1), (2, 2), (1, 0), (3, 0), (2, 0), (0, 0))
FW = 256
LW = GW - FW


def exchange_kernel(
    normed, w, below, row, above, last, q, wbuf, kvs, lasts, qs,
    wsem, xs, xr, ls, lr, qss, qsr, ys, yr,
):
    y, x = place()
    loads = []
    for i, (delta, kind) in enumerate(BLOCKS):
        col = pl.multiple_of(kind * (HEADS * HEAD_DIM) + ((x + delta) % SIDE) * GW, 128)
        load = pltpu.make_async_copy(w.at[:, pl.ds(col, GW)], wbuf.at[i], wsem.at[i])
        load.start()
        loads.append(load)
    barrier = pltpu.get_barrier_semaphore()
    peers = [(0, 1), (0, 2), (0, 3), (1, 0), (3, 0)]
    for dy, dx in peers:
        pl.semaphore_signal(barrier, inc=1, device_id=device(y + dy, x + dx), device_id_type=MESH)
    pl.semaphore_wait(barrier, len(peers))

    def product(i, put):
        loads[i].wait()

        def rows(r, carry):
            at = pl.ds(pl.multiple_of(r * BLK, BLK), BLK)
            value = jnp.dot(normed[at, :], wbuf[i], preferred_element_type=jnp.float32)
            put(at, value)
            return carry

        lax.fori_loop(0, MOSTB, rows, 0)

    def across(src, dst, send, recv, delta):
        return pltpu.make_async_remote_copy(
            src.at[delta], dst.at[delta], send.at[delta], recv.at[delta],
            device_id=device(y, x + delta), device_id_type=MESH,
        )

    first = {delta: across(kvs, row, xs, xr, delta) for delta in (1, 2, 3)}
    later = {delta: across(lasts, last, ls, lr, delta) for delta in (1, 2, 3)}
    query = {delta: across(qs, q, qss, qsr, delta) for delta in (1, 2, 3)}
    sent = []

    def up_down(delta):
        for way, (dy, to) in enumerate(((1, below), (-1, above))):
            copy = pltpu.make_async_remote_copy(
                row.at[delta], to.at[delta], ys.at[way, delta], yr.at[way, delta],
                device_id=device(y + dy, x), device_id_type=MESH,
            )
            copy.start()
            sent.append(copy)

    for i, (delta, kind) in enumerate(BLOCKS):
        if kind == 0:
            to = q if delta == 0 else qs

            def put(at, value, delta=delta, to=to):
                to[delta, at, :] = (value * SCALE).astype(jnp.bfloat16)
        else:
            to, rest = (row, last) if delta == 0 else (kvs, lasts)

            def put(at, value, delta=delta, kind=kind, to=to, rest=rest):
                value = value.astype(jnp.bfloat16)
                to[delta, at, pl.ds((kind - 1) * FW, FW)] = value[:, :FW]
                rest[delta, at, pl.ds((kind - 1) * LW, LW)] = value[:, FW:]

        product(i, put)
        if kind == 2:
            if delta == 0:
                up_down(0)
            elif delta != 2:
                first[delta].start()
    first[1].wait()
    up_down(1)
    first[2].start()
    first[3].wait()
    up_down(3)
    for delta in (1, 3, 2):
        query[delta].start()
    first[2].wait()
    up_down(2)
    for delta in (1, 3, 2):
        later[delta].start()
    for copy in [*query.values(), *later.values(), *sent]:
        copy.wait()


def exchange(normed, w_qkv):
    dma = pltpu.SemaphoreType.DMA
    vmem = pl.BlockSpec(memory_space=pltpu.VMEM)
    shapes = [(SIDE, ROWS, 2 * FW)] * 3 + [(SIDE, ROWS, 2 * LW), (SIDE, ROWS, GW)]
    return pl.pallas_call(
        exchange_kernel,
        out_shape=[jax.ShapeDtypeStruct(shape, jnp.bfloat16) for shape in shapes],
        in_specs=[vmem, pl.BlockSpec(memory_space=pltpu.HBM)],
        out_specs=[vmem] * 5,
        scratch_shapes=[
            pltpu.VMEM((len(BLOCKS), D, GW), jnp.bfloat16),
            pltpu.VMEM((SIDE, ROWS, 2 * FW), jnp.bfloat16),
            pltpu.VMEM((SIDE, ROWS, 2 * LW), jnp.bfloat16),
            pltpu.VMEM((SIDE, ROWS, GW), jnp.bfloat16),
            dma((len(BLOCKS),)),
            *[dma((SIDE,))] * 6,
            dma((2, SIDE)),
            dma((2, SIDE)),
        ],
        compiler_params=pltpu.CompilerParams(
            collective_id=0, has_side_effects=True, vmem_limit_bytes=34 * 2**20
        ),
        name="exchange",
    )(normed, w_qkv)


def attend_kernel(start, pairs, keep, q, below, row, above, out, live, keys, vals, masked, s0, s1, m0, m1, acc):
    y, x = place()
    for k in range(3 * SIDE):
        live[k] = keep[((y + SIDE - 1) * SIDE + k) % (SIDE * SIDE)]
    low = lax.broadcasted_iota(jnp.int32, (1, 128), 1) < HEAD_DIM
    one = jnp.ones((BLK, 128), jnp.bfloat16)
    counts = live
    total = 0
    for k, kv in enumerate((below, row, above)):

        def pack(slot, at, k=k, kv=kv):
            frame, block = slot // MOSTB, slot % MOSTB
            back = (x + SIDE - frame) % SIDE
            used = block < counts[k * SIDE + frame]

            @pl.when(used)
            def _():
                rows = pl.ds(pl.multiple_of(block * BLK, BLK), BLK)
                to = pl.ds(pl.multiple_of(at * BLK, BLK), BLK)
                for c in range(pairs):
                    keys[c, to, :] = kv[back, rows, c * 128 : (c + 1) * 128]
                    v = kv[back, rows, (pairs + c) * 128 : (pairs + c + 1) * 128]
                    vals[c, 0, to, :] = jnp.where(low, v, one)
                    vals[c, 1, to, :] = jnp.where(low, one, v)

            return at + used.astype(jnp.int32)

        total = lax.fori_loop(0, SIDE * MOSTB, pack, total)
    tail = pl.ds(pl.multiple_of(total * BLK, BLK), CH)
    for c in range(pairs):
        keys[c, tail, :] = jnp.zeros((CH, 128), jnp.bfloat16)
        for h in range(2):
            vals[c, h, tail, :] = jnp.zeros((CH, 128), jnp.bfloat16)

    def frame_rows(d, first, blocks, rows):
        full, left = blocks // (CH // BLK), blocks % (CH // BLK)
        for c in range(pairs):
            value = q[d, 0:rows, (start + c) * 128 : (start + c + 1) * 128]
            zero = jnp.zeros_like(value)
            masked[2 * c, 0:rows, :] = jnp.where(low, value, zero)
            masked[2 * c + 1, 0:rows, :] = jnp.where(low, zero, value)

        def span(j, width):
            return (
                pl.ds(pl.multiple_of(first * BLK + j * CH, BLK), width),
                pl.ds(pl.multiple_of(j * CH, BLK), width),
            )

        def score(c, j, width, partial, s, m):
            at, cols = span(j, width)
            for h in range(2):
                value = lax.dot_general(
                    masked[2 * c + h, 0:rows, :], keys[c, at, :],
                    (((1,), (1,)), ((), ())), preferred_element_type=jnp.float32,
                )
                if partial:
                    col = lax.broadcasted_iota(jnp.int32, (1, width), 1)
                    value = jnp.where(col < left * BLK, value, -1e30)
                s[h, 0:rows, cols] = value
                top = m[h, 0:rows, :]
                for t in range(width // 128):
                    top = jnp.maximum(top, value[:, t * 128 : (t + 1) * 128])
                m[h, 0:rows, :] = top

        def weigh(c, j, width, s, m):
            at, cols = span(j, width)
            for h in range(2):
                top = jnp.concatenate([m[h, 0:rows, :]] * (width // 128), axis=1)
                p = jnp.exp2(s[h, 0:rows, cols] - top).astype(jnp.bfloat16)
                acc[h, 0:rows, :] += jnp.dot(p, vals[c, h, at, :], preferred_element_type=jnp.float32)

        bufs = ((s0, m0), (s1, m1))
        for stage in range(pairs + 1):
            s, m = bufs[(stage + 1) % 2]
            sn, mn = bufs[stage % 2]
            if stage:
                m[:, 0:rows, :] = jnp.broadcast_to(
                    jnp.max(m[:, 0:rows, :], axis=2, keepdims=True), (2, rows, 128)
                )
                acc[:, 0:rows, :] = jnp.zeros((2, rows, 128), jnp.float32)
            if stage < pairs:
                mn[:, 0:rows, :] = jnp.full((2, rows, 128), -1e30, jnp.float32)

            def step(j, width, partial, stage=stage, s=s, m=m, sn=sn, mn=mn):
                if stage < pairs:
                    score(stage, j, width, partial, sn, mn)
                if stage:
                    weigh(stage - 1, j, width, s, m)

            lax.fori_loop(0, full, lambda j, t, step=step: (step(j, CH, False), t)[1], 0)

            @pl.when((left > 0) & (left <= CH // BLK // 2))
            def _(step=step):
                step(full, CH // 2, True)

            @pl.when(left > CH // BLK // 2)
            def _(step=step):
                step(full, CH, True)

            if stage:
                even, odd = acc[0, 0:rows, :], acc[1, 0:rows, :]
                even = even / pltpu.roll(even, HEAD_DIM, 1)
                odd = odd / pltpu.roll(odd, HEAD_DIM, 1)
                out[d, 0:rows, (stage - 1) * 128 : stage * 128] = jnp.where(low, even, odd).astype(jnp.bfloat16)

    def frame_body(f, first):
        blocks = counts[f]
        for k in range(1, 2 * SIDE + 1):
            blocks += counts[f + k]
        own = counts[SIDE + f]
        d = (x + SIDE - f) % SIDE
        for n in range(1, MOSTB + 1):

            @pl.when(own == n)
            def _(n=n):
                frame_rows(d, first, blocks, n * BLK)
                if n < MOSTB:
                    out[d, n * BLK :, :] = jnp.zeros((ROWS - n * BLK, pairs * 128), jnp.bfloat16)

        return first + counts[f]

    lax.fori_loop(0, SIDE, frame_body, 0)


def attend(start, pairs, keep_count, q, below, row, above):
    vmem = pl.BlockSpec(memory_space=pltpu.VMEM)
    return pl.pallas_call(
        functools.partial(attend_kernel, start, pairs),
        out_shape=jax.ShapeDtypeStruct((SIDE, ROWS, pairs * 128), jnp.bfloat16),
        in_specs=[pl.BlockSpec(memory_space=pltpu.SMEM)] + [vmem] * 4,
        out_specs=vmem,
        scratch_shapes=[
            pltpu.SMEM((3 * SIDE,), jnp.int32),
            pltpu.VMEM((pairs, KROWS, 128), jnp.bfloat16),
            pltpu.VMEM((pairs, 2, KROWS, 128), jnp.bfloat16),
            pltpu.VMEM((2 * pairs, ROWS, 128), jnp.bfloat16),
            pltpu.VMEM((2, ROWS, WINDOW), jnp.float32),
            pltpu.VMEM((2, ROWS, WINDOW), jnp.float32),
            *[pltpu.VMEM((2, ROWS, 128), jnp.float32)] * 3,
        ],
        compiler_params=pltpu.CompilerParams(vmem_limit_bytes=42 * 2**20),
        cost_estimate=pl.CostEstimate(
            flops=pairs * 18 * 10**9, bytes_accessed=pairs * 2**21, transcendentals=0
        ),
        name="attend",
    )(keep_count, q, below, row, above)


def project_kernel(own, one, two, three, rest, w, out, got, wbuf, total, wsem, ss, rs):
    y, x = place()
    order = (0, 1, 3, 2)
    loads = []
    for i, delta in enumerate(order):
        row = pl.multiple_of(((x - delta) % SIDE) * GW, GW)
        load = pltpu.make_async_copy(w.at[pl.ds(row, GW), :], wbuf.at[i], wsem.at[i])
        load.start()
        loads.append(load)
    barrier = pltpu.get_barrier_semaphore()
    for delta in (1, 2, 3):
        pl.semaphore_signal(barrier, inc=1, device_id=device(y, x + delta), device_id_type=MESH)
    pl.semaphore_wait(barrier, 3)
    copies = {}
    for delta in (2, 1, 3):
        copies[delta] = pltpu.make_async_remote_copy(
            rest.at[(SIDE - delta) % SIDE], got.at[delta], ss.at[delta], rs.at[delta],
            device_id=device(y, x + delta), device_id_type=MESH,
        )
        copies[delta].start()
    parts = (own, one, two, three)
    for i, delta in enumerate(order):
        loads[i].wait()

        def first(r, carry, i=i, delta=delta):
            at = pl.ds(pl.multiple_of(r * BLK, BLK), BLK)
            value = jnp.dot(parts[delta][at, :], wbuf[i, :FW, :], preferred_element_type=jnp.float32)
            if i == 0:
                value += jnp.dot(rest[0, at, :], wbuf[i, FW:, :], preferred_element_type=jnp.float32)
            else:
                value += total[at, :]
            total[at, :] = value
            return carry

        lax.fori_loop(0, MOSTB, first, 0)
    for i, delta in enumerate(order):
        if delta == 0:
            continue
        copies[delta].wait()

        def rows(r, carry, i=i, delta=delta):
            at = pl.ds(pl.multiple_of(r * BLK, BLK), BLK)
            value = total[at, :]
            value += jnp.dot(got[delta, at, :], wbuf[i, FW:, :], preferred_element_type=jnp.float32)
            if i < SIDE - 1:
                total[at, :] = value
            else:
                scale = lax.rsqrt(jnp.mean(value * value, axis=-1, keepdims=True) + 1e-06)
                out[at, :] = (value * scale).astype(jnp.bfloat16)
            return carry

        lax.fori_loop(0, MOSTB, rows, 0)


def project(parts, rest, w_out):
    dma = pltpu.SemaphoreType.DMA
    vmem = pl.BlockSpec(memory_space=pltpu.VMEM)
    return pl.pallas_call(
        project_kernel,
        out_shape=jax.ShapeDtypeStruct((ROWS, D), jnp.bfloat16),
        in_specs=[vmem] * 5 + [pl.BlockSpec(memory_space=pltpu.HBM)],
        out_specs=vmem,
        scratch_shapes=[
            pltpu.VMEM((SIDE, ROWS, LW), jnp.bfloat16),
            pltpu.VMEM((SIDE, GW, D), jnp.bfloat16),
            pltpu.VMEM((ROWS, D), jnp.float32),
            *[dma((SIDE,))] * 3,
        ],
        compiler_params=pltpu.CompilerParams(
            collective_id=1, has_side_effects=True, vmem_limit_bytes=24 * 2**20
        ),
        name="project",
    )(*parts, rest, w_out)


def scatter_kernel(order, count, block, out, zero, sems):
    own = count[lax.axis_index("frame")]
    zero[...] = jnp.zeros_like(zero)

    def each(act):
        for j in range(order.shape[1]):
            rows = pl.ds(pl.multiple_of(order[0, j] * BLK, BLK), BLK)
            if j == MOSTB:
                act(pltpu.make_async_copy(zero, out.at[rows, :], sems.at[j]))
                continue

            @pl.when(j < own)
            def _(j=j, rows=rows):
                act(pltpu.make_async_copy(block.at[pl.ds(j * BLK, BLK), :], out.at[rows, :], sems.at[j]))

            @pl.when(j >= own)
            def _(j=j, rows=rows):
                act(pltpu.make_async_copy(zero, out.at[rows, :], sems.at[j]))

    each(lambda copy: copy.start())
    each(lambda copy: copy.wait())


def scatter(keep_order, keep_count, normalized):
    blocks = keep_order.shape[1]
    smem = pl.BlockSpec(memory_space=pltpu.SMEM)
    return pl.pallas_call(
        scatter_kernel,
        in_specs=[smem, smem, pl.BlockSpec(memory_space=pltpu.VMEM)],
        out_specs=pl.BlockSpec(memory_space=pl.ANY),
        out_shape=jax.ShapeDtypeStruct((blocks * BLK, D), jnp.bfloat16),
        scratch_shapes=[pltpu.VMEM((BLK, D), jnp.bfloat16), pltpu.SemaphoreType.DMA((blocks,))],
        compiler_params=pltpu.CompilerParams(vmem_limit_bytes=8 * 2**20),
        name="scatter",
    )(keep_order, keep_count, normalized)


def shifted(value, dy, dx):
    def to(f):
        return (f // SIDE + dy) % SIDE * SIDE + (f + dx) % SIDE

    return lax.ppermute(value, "frame", [(f, to(f)) for f in range(SIDE * SIDE)])


def shards(tokens, keep_count, keep_order, w_qkv, w_out):
    normed = norm_kept(keep_order, tokens)
    below, row, above, last, q = exchange(normed, w_qkv)
    last_below = shifted(last, 1, 0)
    last_above = shifted(last, -1, 0)
    part = attend(0, 2, keep_count, q, below, row, above)
    parts = [shifted(part[(SIDE - dx) % SIDE], 0, dx) if dx else part[0] for dx in range(SIDE)]
    rest = attend(2, 1, keep_count, q, last_below, last, last_above)
    normalized = project(parts, rest, w_out)
    return scatter(keep_order, keep_count, normalized)


def solution(mesh):
    return jax.shard_map(
        shards,
        mesh=mesh,
        in_specs=(P(("orbit", "frame"), None), P("orbit"), P(("orbit", "frame"), None), P(), P()),
        out_specs=P(("orbit", "frame"), None),
        check_vma=False,
    )
```

```python
import functools

import jax
import jax.numpy as jnp
from jax import lax
from jax.experimental import pallas as pl
from jax.experimental.pallas import tpu as pltpu
from jax.sharding import PartitionSpec as P

D = 1536
HEADS = 24
HEAD_DIM = 64
BLK = 128
MOSTB = 3
ROWS = MOSTB * BLK
SIDE = 4
GW = 384
CH = 1024
WINDOW = 28 * BLK
BEGUN_WINDOW = 16 * BLK
KROWS = 36 * BLK + CH
SCALE = HEAD_DIM ** (-0.5) * 1.4426950408889634
MESH = pl.DeviceIdType.MESH


def place():
    me = lax.axis_index("frame")
    return me // SIDE, me % SIDE


def device(y, x):
    return {"frame": (y % SIDE) * SIDE + x % SIDE}


def norm_kernel(order, tokens, out, kept, sems):
    loads = []
    for j in range(MOSTB):
        rows = pl.ds(pl.multiple_of(order[0, j] * BLK, BLK), BLK)
        loads.append(pltpu.make_async_copy(tokens.at[rows, :], kept.at[j], sems.at[j]))
        loads[j].start()
    for j in range(MOSTB):
        loads[j].wait()
        wide = kept[j].astype(jnp.float32)
        scale = lax.rsqrt(jnp.mean(wide * wide, axis=-1, keepdims=True) + 1e-06)
        out[j * BLK : (j + 1) * BLK, :] = (wide * scale).astype(jnp.bfloat16)


def norm_kept(keep_order, tokens):
    return pl.pallas_call(
        norm_kernel,
        in_specs=[pl.BlockSpec(memory_space=pltpu.SMEM), pl.BlockSpec(memory_space=pltpu.HBM)],
        out_specs=pl.BlockSpec(memory_space=pltpu.VMEM),
        out_shape=jax.ShapeDtypeStruct((ROWS, D), jnp.bfloat16),
        scratch_shapes=[pltpu.VMEM((MOSTB, BLK, D), jnp.bfloat16), pltpu.SemaphoreType.DMA((MOSTB,))],
        compiler_params=pltpu.CompilerParams(vmem_limit_bytes=12 * 2**20),
        name="norm_kept",
    )(keep_order, tokens)


BLOCKS = ((1, 1), (1, 2), (0, 1), (0, 2), (3, 1), (3, 2), (2, 1), (2, 2), (1, 0), (3, 0), (2, 0), (0, 0))
FW = 256
LW = GW - FW


def exchange_kernel(
    keep, normed, w, below, row, above, last, q, tops, sums, wbuf, kvs, lasts, qs,
    wsem, xs, xr, ls, lr, qss, qsr, rss, rsr, ys, yr,
):
    y, x = place()
    loads = []
    for i, (delta, kind) in enumerate(BLOCKS):
        col = pl.multiple_of(kind * (HEADS * HEAD_DIM) + ((x + delta) % SIDE) * GW, 128)
        load = pltpu.make_async_copy(w.at[:, pl.ds(col, GW)], wbuf.at[i], wsem.at[i])
        load.start()
        loads.append(load)
    barrier = pltpu.get_barrier_semaphore()
    peers = [(0, 1), (0, 2), (0, 3), (1, 0), (3, 0)]
    for dy, dx in peers:
        pl.semaphore_signal(barrier, inc=1, device_id=device(y + dy, x + dx), device_id_type=MESH)
    pl.semaphore_wait(barrier, len(peers))

    def product(i, put):
        loads[i].wait()

        def rows(r, carry):
            at = pl.ds(pl.multiple_of(r * BLK, BLK), BLK)
            value = jnp.dot(normed[at, :], wbuf[i], preferred_element_type=jnp.float32)
            put(at, value)
            return carry

        lax.fori_loop(0, MOSTB, rows, 0)

    def across(src, dst, send, recv, delta):
        return pltpu.make_async_remote_copy(
            src.at[delta], dst.at[delta], send.at[delta], recv.at[delta],
            device_id=device(y, x + delta), device_id_type=MESH,
        )

    first = {delta: across(kvs, row, xs, xr, delta) for delta in (1, 2, 3)}
    later = {delta: across(lasts, last, ls, lr, delta) for delta in (1, 2, 3)}
    part, rest = (slice(None), slice(None), pl.ds(0, FW)), (slice(None), slice(None), pl.ds(FW, LW))
    query = {delta: across(qs.at[part], q.at[part], qss, qsr, delta) for delta in (1, 2, 3)}
    query_later = {delta: across(qs.at[rest], q.at[rest], rss, rsr, delta) for delta in (1, 2, 3)}
    sent = []

    def up_down(delta):
        for way, (dy, to) in enumerate(((1, below), (-1, above))):
            copy = pltpu.make_async_remote_copy(
                row.at[delta], to.at[delta], ys.at[way, delta], yr.at[way, delta],
                device_id=device(y + dy, x), device_id_type=MESH,
            )
            copy.start()
            sent.append(copy)

    for i, (delta, kind) in enumerate(BLOCKS):
        if kind == 0:
            to = q if delta == 0 else qs

            def put(at, value, delta=delta, to=to):
                to[delta, at, :] = (value * SCALE).astype(jnp.bfloat16)
        else:
            to, rest = (row, last) if delta == 0 else (kvs, lasts)

            def put(at, value, delta=delta, kind=kind, to=to, rest=rest):
                value = value.astype(jnp.bfloat16)
                to[delta, at, pl.ds((kind - 1) * FW, FW)] = value[:, :FW]
                rest[delta, at, pl.ds((kind - 1) * LW, LW)] = value[:, FW:]

        product(i, put)
        if kind == 2:
            if delta == 0:
                up_down(0)
            elif delta != 2:
                first[delta].start()
    first[1].wait()
    up_down(1)
    first[2].start()
    first[3].wait()
    up_down(3)
    for delta in (1, 3, 2):
        query[delta].start()
    first[2].wait()
    up_down(2)
    for delta in (1, 3, 2):
        later[delta].start()
    for delta in (1, 3, 2):
        query_later[delta].start()
    live = [keep[y * SIDE + (x + SIDE - back) % SIDE] * BLK for back in range(SIDE)]
    low = lax.broadcasted_iota(jnp.int32, (1, 128), 1) < HEAD_DIM
    col = lax.broadcasted_iota(jnp.int32, (1, ROWS), 1)
    ones = jnp.ones((ROWS, 128), jnp.bfloat16)

    def own_row(d):
        def pair(c, carry):
            at = pl.ds(pl.multiple_of(c * 128, 128), 128)
            value_at = pl.ds(pl.multiple_of(FW + c * 128, 128), 128)
            for h in range(2):
                own = low if h == 0 else jnp.logical_not(low)
                value = q[d, :, at]
                value = jnp.where(own, value, jnp.zeros_like(value))
                scores = []
                top = None
                for back in range(SIDE):
                    score = lax.dot_general(
                        value, row[back, :, at], (((1,), (1,)), ((), ())),
                        preferred_element_type=jnp.float32,
                    )
                    score = jnp.where(col < live[back], score, -1e30)
                    scores.append(score)
                    for t in range(MOSTB):
                        piece = score[:, t * 128 : (t + 1) * 128]
                        top = piece if top is None else jnp.maximum(top, piece)
                top = jnp.broadcast_to(jnp.max(top, axis=1, keepdims=True), (ROWS, 128))
                wide = jnp.concatenate([top] * MOSTB, axis=1)
                total = None
                for back in range(SIDE):
                    p = jnp.exp2(scores[back] - wide).astype(jnp.bfloat16)
                    v = jnp.where(own, row[back, :, value_at], ones)
                    o = jnp.dot(p, v, preferred_element_type=jnp.float32)
                    total = o if total is None else total + o
                tops[d, c, h] = top
                sums[d, c, h] = total
            return carry

        lax.fori_loop(0, FW // 128, pair, 0)

    own_row(0)
    for delta in (1, 3, 2):
        query[delta].wait()
        own_row(delta)
    for copy in [*later.values(), *query_later.values(), *sent]:
        copy.wait()


def exchange(keep_count, normed, w_qkv):
    dma = pltpu.SemaphoreType.DMA
    vmem = pl.BlockSpec(memory_space=pltpu.VMEM)
    shapes = [(SIDE, ROWS, 2 * FW)] * 3 + [(SIDE, ROWS, 2 * LW), (SIDE, ROWS, GW)]
    return pl.pallas_call(
        exchange_kernel,
        out_shape=[jax.ShapeDtypeStruct(shape, jnp.bfloat16) for shape in shapes]
        + [jax.ShapeDtypeStruct((SIDE, FW // 128, 2, ROWS, 128), jnp.float32)] * 2,
        in_specs=[pl.BlockSpec(memory_space=pltpu.SMEM), vmem, pl.BlockSpec(memory_space=pltpu.HBM)],
        out_specs=[vmem] * 7,
        scratch_shapes=[
            pltpu.VMEM((len(BLOCKS), D, GW), jnp.bfloat16),
            pltpu.VMEM((SIDE, ROWS, 2 * FW), jnp.bfloat16),
            pltpu.VMEM((SIDE, ROWS, 2 * LW), jnp.bfloat16),
            pltpu.VMEM((SIDE, ROWS, GW), jnp.bfloat16),
            dma((len(BLOCKS),)),
            *[dma((SIDE,))] * 8,
            dma((2, SIDE)),
            dma((2, SIDE)),
        ],
        compiler_params=pltpu.CompilerParams(
            collective_id=0, has_side_effects=True, vmem_limit_bytes=36 * 2**20
        ),
        name="exchange",
    )(keep_count, normed, w_qkv)


def attend_kernel(start, pairs, begun, keep, q, *refs):
    if begun:
        below, above, tops, sums = refs[:4]
        sources = ((0, below), (2, above))
    else:
        below, row, above = refs[:3]
        sources = ((0, below), (1, row), (2, above))
    out, live, keys, vals, masked, s0, s1, m0, m1, acc = refs[4 if begun else 3 :]
    y, x = place()
    for k, (dy, _) in enumerate(sources):
        for frame in range(SIDE):
            live[k * SIDE + frame] = keep[((y + SIDE - 1 + dy) % SIDE) * SIDE + frame]
    low = lax.broadcasted_iota(jnp.int32, (1, 128), 1) < HEAD_DIM
    one = jnp.ones((BLK, 128), jnp.bfloat16)
    counts = live
    total = 0
    for k, (_, kv) in enumerate(sources):

        def pack(slot, at, k=k, kv=kv):
            frame, block = slot // MOSTB, slot % MOSTB
            back = (x + SIDE - frame) % SIDE
            used = block < counts[k * SIDE + frame]

            @pl.when(used)
            def _():
                rows = pl.ds(pl.multiple_of(block * BLK, BLK), BLK)
                to = pl.ds(pl.multiple_of(at * BLK, BLK), BLK)
                for c in range(pairs):
                    keys[c, to, :] = kv[back, rows, c * 128 : (c + 1) * 128]
                    v = kv[back, rows, (pairs + c) * 128 : (pairs + c + 1) * 128]
                    vals[c, 0, to, :] = jnp.where(low, v, one)
                    vals[c, 1, to, :] = jnp.where(low, one, v)

            return at + used.astype(jnp.int32)

        total = lax.fori_loop(0, SIDE * MOSTB, pack, total)
    tail = pl.ds(pl.multiple_of(total * BLK, BLK), CH)
    for c in range(pairs):
        keys[c, tail, :] = jnp.zeros((CH, 128), jnp.bfloat16)
        for h in range(2):
            vals[c, h, tail, :] = jnp.zeros((CH, 128), jnp.bfloat16)

    def frame_rows(d, first, blocks, rows):
        full, left = blocks // (CH // BLK), blocks % (CH // BLK)
        for c in range(pairs):
            value = q[d, 0:rows, (start + c) * 128 : (start + c + 1) * 128]
            zero = jnp.zeros_like(value)
            masked[2 * c, 0:rows, :] = jnp.where(low, value, zero)
            masked[2 * c + 1, 0:rows, :] = jnp.where(low, zero, value)

        def span(j, width):
            return (
                pl.ds(pl.multiple_of(first * BLK + j * CH, BLK), width),
                pl.ds(pl.multiple_of(j * CH, BLK), width),
            )

        def score(c, j, width, partial, s, m):
            at, cols = span(j, width)
            for h in range(2):
                value = lax.dot_general(
                    masked[2 * c + h, 0:rows, :], keys[c, at, :],
                    (((1,), (1,)), ((), ())), preferred_element_type=jnp.float32,
                )
                if partial:
                    col = lax.broadcasted_iota(jnp.int32, (1, width), 1)
                    value = jnp.where(col < left * BLK, value, -1e30)
                s[h, 0:rows, cols] = value
                top = m[h, 0:rows, :]
                for t in range(width // 128):
                    top = jnp.maximum(top, value[:, t * 128 : (t + 1) * 128])
                m[h, 0:rows, :] = top

        def weigh(c, j, width, s, m):
            at, cols = span(j, width)
            for h in range(2):
                top = jnp.concatenate([m[h, 0:rows, :]] * (width // 128), axis=1)
                p = jnp.exp2(s[h, 0:rows, cols] - top).astype(jnp.bfloat16)
                acc[h, 0:rows, :] += jnp.dot(p, vals[c, h, at, :], preferred_element_type=jnp.float32)

        bufs = ((s0, m0), (s1, m1))
        for stage in range(pairs + 1):
            s, m = bufs[(stage + 1) % 2]
            sn, mn = bufs[stage % 2]
            if stage:
                top = jnp.broadcast_to(
                    jnp.max(m[:, 0:rows, :], axis=2, keepdims=True), (2, rows, 128)
                )
                if begun:
                    before = tops[d, stage - 1, :, 0:rows, :]
                    top = jnp.maximum(top, before)
                    acc[:, 0:rows, :] = sums[d, stage - 1, :, 0:rows, :] * jnp.exp2(before - top)
                else:
                    acc[:, 0:rows, :] = jnp.zeros((2, rows, 128), jnp.float32)
                m[:, 0:rows, :] = top
            if stage < pairs:
                mn[:, 0:rows, :] = jnp.full((2, rows, 128), -1e30, jnp.float32)

            def step(j, width, partial, stage=stage, s=s, m=m, sn=sn, mn=mn):
                if stage < pairs:
                    score(stage, j, width, partial, sn, mn)
                if stage:
                    weigh(stage - 1, j, width, s, m)

            lax.fori_loop(0, full, lambda j, t, step=step: (step(j, CH, False), t)[1], 0)

            @pl.when((left > 0) & (left <= CH // BLK // 2))
            def _(step=step):
                step(full, CH // 2, True)

            @pl.when(left > CH // BLK // 2)
            def _(step=step):
                step(full, CH, True)

            if stage:
                even, odd = acc[0, 0:rows, :], acc[1, 0:rows, :]
                even = even / pltpu.roll(even, HEAD_DIM, 1)
                odd = odd / pltpu.roll(odd, HEAD_DIM, 1)
                out[d, 0:rows, (stage - 1) * 128 : stage * 128] = jnp.where(low, even, odd).astype(jnp.bfloat16)

    def frame_body(f, first):
        blocks = counts[f]
        for k in range(1, len(sources) * SIDE - SIDE + 1):
            blocks += counts[f + k]
        own = keep[y * SIDE + f]
        d = (x + SIDE - f) % SIDE
        for n in range(1, MOSTB + 1):

            @pl.when(own == n)
            def _(n=n):
                frame_rows(d, first, blocks, n * BLK)
                if n < MOSTB:
                    out[d, n * BLK :, :] = jnp.zeros((ROWS - n * BLK, pairs * 128), jnp.bfloat16)

        return first + counts[f]

    lax.fori_loop(0, SIDE, frame_body, 0)


def attend(start, pairs, begun, keep_count, q, *rest):
    window = BEGUN_WINDOW if begun else WINDOW
    vmem = pl.BlockSpec(memory_space=pltpu.VMEM)
    return pl.pallas_call(
        functools.partial(attend_kernel, start, pairs, begun),
        out_shape=jax.ShapeDtypeStruct((SIDE, ROWS, pairs * 128), jnp.bfloat16),
        in_specs=[pl.BlockSpec(memory_space=pltpu.SMEM)] + [vmem] * (1 + len(rest)),
        out_specs=vmem,
        scratch_shapes=[
            pltpu.SMEM((3 * SIDE,), jnp.int32),
            pltpu.VMEM((pairs, KROWS, 128), jnp.bfloat16),
            pltpu.VMEM((pairs, 2, KROWS, 128), jnp.bfloat16),
            pltpu.VMEM((2 * pairs, ROWS, 128), jnp.bfloat16),
            pltpu.VMEM((2, ROWS, window), jnp.float32),
            pltpu.VMEM((2, ROWS, window), jnp.float32),
            *[pltpu.VMEM((2, ROWS, 128), jnp.float32)] * 3,
        ],
        compiler_params=pltpu.CompilerParams(vmem_limit_bytes=(32 if begun else 36) * 2**20),
        cost_estimate=pl.CostEstimate(
            flops=pairs * 18 * 10**9, bytes_accessed=pairs * 2**21, transcendentals=0
        ),
        name="attend",
    )(keep_count, q, *rest)


def project_kernel(own, one, two, three, rest, w, out, got, wbuf, total, wsem, ss, rs):
    y, x = place()
    order = (0, 1, 3, 2)
    loads = []
    for i, delta in enumerate(order):
        row = pl.multiple_of(((x - delta) % SIDE) * GW, GW)
        load = pltpu.make_async_copy(w.at[pl.ds(row, GW), :], wbuf.at[i], wsem.at[i])
        load.start()
        loads.append(load)
    barrier = pltpu.get_barrier_semaphore()
    for delta in (1, 2, 3):
        pl.semaphore_signal(barrier, inc=1, device_id=device(y, x + delta), device_id_type=MESH)
    pl.semaphore_wait(barrier, 3)
    copies = {}
    for delta in (2, 1, 3):
        copies[delta] = pltpu.make_async_remote_copy(
            rest.at[(SIDE - delta) % SIDE], got.at[delta], ss.at[delta], rs.at[delta],
            device_id=device(y, x + delta), device_id_type=MESH,
        )
        copies[delta].start()
    parts = (own, one, two, three)
    for i, delta in enumerate(order):
        loads[i].wait()

        def first(r, carry, i=i, delta=delta):
            at = pl.ds(pl.multiple_of(r * BLK, BLK), BLK)
            value = jnp.dot(parts[delta][at, :], wbuf[i, :FW, :], preferred_element_type=jnp.float32)
            if i == 0:
                value += jnp.dot(rest[0, at, :], wbuf[i, FW:, :], preferred_element_type=jnp.float32)
            else:
                value += total[at, :]
            total[at, :] = value
            return carry

        lax.fori_loop(0, MOSTB, first, 0)
    for i, delta in enumerate(order):
        if delta == 0:
            continue
        copies[delta].wait()

        def rows(r, carry, i=i, delta=delta):
            at = pl.ds(pl.multiple_of(r * BLK, BLK), BLK)
            value = total[at, :]
            value += jnp.dot(got[delta, at, :], wbuf[i, FW:, :], preferred_element_type=jnp.float32)
            if i < SIDE - 1:
                total[at, :] = value
            else:
                scale = lax.rsqrt(jnp.mean(value * value, axis=-1, keepdims=True) + 1e-06)
                out[at, :] = (value * scale).astype(jnp.bfloat16)
            return carry

        lax.fori_loop(0, MOSTB, rows, 0)


def project(parts, rest, w_out):
    dma = pltpu.SemaphoreType.DMA
    vmem = pl.BlockSpec(memory_space=pltpu.VMEM)
    return pl.pallas_call(
        project_kernel,
        out_shape=jax.ShapeDtypeStruct((ROWS, D), jnp.bfloat16),
        in_specs=[vmem] * 5 + [pl.BlockSpec(memory_space=pltpu.HBM)],
        out_specs=vmem,
        scratch_shapes=[
            pltpu.VMEM((SIDE, ROWS, LW), jnp.bfloat16),
            pltpu.VMEM((SIDE, GW, D), jnp.bfloat16),
            pltpu.VMEM((ROWS, D), jnp.float32),
            *[dma((SIDE,))] * 3,
        ],
        compiler_params=pltpu.CompilerParams(
            collective_id=1, has_side_effects=True, vmem_limit_bytes=24 * 2**20
        ),
        name="project",
    )(*parts, rest, w_out)


def scatter_kernel(order, count, block, out, zero, sems):
    own = count[lax.axis_index("frame")]
    zero[...] = jnp.zeros_like(zero)

    def each(act):
        for j in range(order.shape[1]):
            rows = pl.ds(pl.multiple_of(order[0, j] * BLK, BLK), BLK)
            if j == MOSTB:
                act(pltpu.make_async_copy(zero, out.at[rows, :], sems.at[j]))
                continue

            @pl.when(j < own)
            def _(j=j, rows=rows):
                act(pltpu.make_async_copy(block.at[pl.ds(j * BLK, BLK), :], out.at[rows, :], sems.at[j]))

            @pl.when(j >= own)
            def _(j=j, rows=rows):
                act(pltpu.make_async_copy(zero, out.at[rows, :], sems.at[j]))

    each(lambda copy: copy.start())
    each(lambda copy: copy.wait())


def scatter(keep_order, keep_count, normalized):
    blocks = keep_order.shape[1]
    smem = pl.BlockSpec(memory_space=pltpu.SMEM)
    return pl.pallas_call(
        scatter_kernel,
        in_specs=[smem, smem, pl.BlockSpec(memory_space=pltpu.VMEM)],
        out_specs=pl.BlockSpec(memory_space=pl.ANY),
        out_shape=jax.ShapeDtypeStruct((blocks * BLK, D), jnp.bfloat16),
        scratch_shapes=[pltpu.VMEM((BLK, D), jnp.bfloat16), pltpu.SemaphoreType.DMA((blocks,))],
        compiler_params=pltpu.CompilerParams(vmem_limit_bytes=8 * 2**20),
        name="scatter",
    )(keep_order, keep_count, normalized)


def shifted(value, dy, dx):
    def to(f):
        return (f // SIDE + dy) % SIDE * SIDE + (f + dx) % SIDE

    return lax.ppermute(value, "frame", [(f, to(f)) for f in range(SIDE * SIDE)])


def shards(tokens, keep_count, keep_order, w_qkv, w_out):
    normed = norm_kept(keep_order, tokens)
    below, row, above, last, q, tops, sums = exchange(keep_count, normed, w_qkv)
    last_below = shifted(last, 1, 0)
    last_above = shifted(last, -1, 0)
    part = attend(0, 2, True, keep_count, q, below, above, tops, sums)
    parts = [shifted(part[(SIDE - dx) % SIDE], 0, dx) if dx else part[0] for dx in range(SIDE)]
    rest = attend(2, 1, False, keep_count, q, last_below, last, last_above)
    normalized = project(parts, rest, w_out)
    return scatter(keep_order, keep_count, normalized)


def solution(mesh):
    return jax.shard_map(
        shards,
        mesh=mesh,
        in_specs=(P(("orbit", "frame"), None), P("orbit"), P(("orbit", "frame"), None), P(), P()),
        out_specs=P(("orbit", "frame"), None),
        check_vma=False,
    )
```

```python
import functools

import jax
import jax.numpy as jnp
from jax import lax
from jax.experimental import pallas as pl
from jax.experimental.pallas import tpu as pltpu
from jax.sharding import PartitionSpec as P

D = 1536
HEADS = 24
HEAD_DIM = 64
BLK = 128
MOSTB = 3
ROWS = MOSTB * BLK
SIDE = 4
GW = 384
CH = 1024
WINDOW = 28 * BLK
BEGUN_WINDOW = 16 * BLK
KROWS = 36 * BLK + CH
SCALE = HEAD_DIM ** (-0.5) * 1.4426950408889634
MESH = pl.DeviceIdType.MESH


def place():
    me = lax.axis_index("frame")
    return me // SIDE, me % SIDE


def device(y, x):
    return {"frame": (y % SIDE) * SIDE + x % SIDE}


def norm_kernel(order, tokens, out, kept, sems):
    loads = []
    for j in range(MOSTB):
        rows = pl.ds(pl.multiple_of(order[0, j] * BLK, BLK), BLK)
        loads.append(pltpu.make_async_copy(tokens.at[rows, :], kept.at[j], sems.at[j]))
        loads[j].start()
    for j in range(MOSTB):
        loads[j].wait()
        wide = kept[j].astype(jnp.float32)
        scale = lax.rsqrt(jnp.mean(wide * wide, axis=-1, keepdims=True) + 1e-06)
        out[j * BLK : (j + 1) * BLK, :] = (wide * scale).astype(jnp.bfloat16)


def norm_kept(keep_order, tokens):
    return pl.pallas_call(
        norm_kernel,
        in_specs=[pl.BlockSpec(memory_space=pltpu.SMEM), pl.BlockSpec(memory_space=pltpu.HBM)],
        out_specs=pl.BlockSpec(memory_space=pltpu.VMEM),
        out_shape=jax.ShapeDtypeStruct((ROWS, D), jnp.bfloat16),
        scratch_shapes=[pltpu.VMEM((MOSTB, BLK, D), jnp.bfloat16), pltpu.SemaphoreType.DMA((MOSTB,))],
        compiler_params=pltpu.CompilerParams(vmem_limit_bytes=12 * 2**20),
        name="norm_kept",
    )(keep_order, tokens)


BLOCKS = ((1, 1), (1, 2), (0, 1), (0, 2), (3, 1), (3, 2), (2, 1), (2, 2), (1, 0), (3, 0), (2, 0), (0, 0))
FW = 256
LW = GW - FW


def exchange_kernel(
    keep, normed, w, below, row, above, last, q, tops, sums, wbuf, kvs, lasts, qs,
    wsem, xs, xr, ls, lr, qss, qsr, rss, rsr, ys, yr,
):
    y, x = place()
    loads = []
    for i, (delta, kind) in enumerate(BLOCKS):
        col = pl.multiple_of(kind * (HEADS * HEAD_DIM) + ((x + delta) % SIDE) * GW, 128)
        load = pltpu.make_async_copy(w.at[:, pl.ds(col, GW)], wbuf.at[i], wsem.at[i])
        load.start()
        loads.append(load)
    barrier = pltpu.get_barrier_semaphore()
    peers = [(0, 1), (0, 2), (0, 3), (1, 0), (3, 0)]
    for dy, dx in peers:
        pl.semaphore_signal(barrier, inc=1, device_id=device(y + dy, x + dx), device_id_type=MESH)
    pl.semaphore_wait(barrier, len(peers))

    def product(i, put):
        loads[i].wait()

        def rows(r, carry):
            at = pl.ds(pl.multiple_of(r * BLK, BLK), BLK)
            value = jnp.dot(normed[at, :], wbuf[i], preferred_element_type=jnp.float32)
            put(at, value)
            return carry

        lax.fori_loop(0, MOSTB, rows, 0)

    def across(src, dst, send, recv, delta):
        return pltpu.make_async_remote_copy(
            src.at[delta], dst.at[delta], send.at[delta], recv.at[delta],
            device_id=device(y, x + delta), device_id_type=MESH,
        )

    first = {delta: across(kvs, row, xs, xr, delta) for delta in (1, 2, 3)}
    later = {delta: across(lasts, last, ls, lr, delta) for delta in (1, 2, 3)}
    part, rest = (slice(None), slice(None), pl.ds(0, FW)), (slice(None), slice(None), pl.ds(FW, LW))
    query = {delta: across(qs.at[part], q.at[part], qss, qsr, delta) for delta in (1, 2, 3)}
    query_later = {delta: across(qs.at[rest], q.at[rest], rss, rsr, delta) for delta in (1, 2, 3)}
    sent = []

    def up_down(delta):
        for way, (dy, to) in enumerate(((1, below), (-1, above))):
            copy = pltpu.make_async_remote_copy(
                row.at[delta], to.at[delta], ys.at[way, delta], yr.at[way, delta],
                device_id=device(y + dy, x), device_id_type=MESH,
            )
            copy.start()
            sent.append(copy)

    for i, (delta, kind) in enumerate(BLOCKS):
        if kind == 0:
            to = q if delta == 0 else qs

            def put(at, value, delta=delta, to=to):
                to[delta, at, :] = (value * SCALE).astype(jnp.bfloat16)
        else:
            to, rest = (row, last) if delta == 0 else (kvs, lasts)

            def put(at, value, delta=delta, kind=kind, to=to, rest=rest):
                value = value.astype(jnp.bfloat16)
                to[delta, at, pl.ds((kind - 1) * FW, FW)] = value[:, :FW]
                rest[delta, at, pl.ds((kind - 1) * LW, LW)] = value[:, FW:]

        product(i, put)
        if kind == 2:
            if delta == 0:
                up_down(0)
            else:
                first[delta].start()
    first[1].wait()
    up_down(1)
    first[3].wait()
    up_down(3)
    for delta in (1, 3, 2):
        query[delta].start()
    first[2].wait()
    up_down(2)
    for delta in (1, 3, 2):
        later[delta].start()
    for delta in (1, 3, 2):
        query_later[delta].start()
    live = [keep[y * SIDE + (x + SIDE - back) % SIDE] * BLK for back in range(SIDE)]
    low = lax.broadcasted_iota(jnp.int32, (1, 128), 1) < HEAD_DIM
    col = lax.broadcasted_iota(jnp.int32, (1, ROWS), 1)
    ones = jnp.ones((ROWS, 128), jnp.bfloat16)

    def own_row(i, carry):
        d, c = i // (FW // 128), i % (FW // 128)

        @pl.when((d > 0) & (c == 0))
        def _():
            across(qs.at[part], q.at[part], qss, qsr, d).wait()

        at = pl.ds(pl.multiple_of(c * 128, 128), 128)
        value_at = pl.ds(pl.multiple_of(FW + c * 128, 128), 128)
        masks = (low, jnp.logical_not(low))
        query_pair = q[d, :, at]
        scores, highest = [], []
        for h in range(2):
            value = jnp.where(masks[h], query_pair, jnp.zeros_like(query_pair))
            rowed = []
            top = None
            for back in range(SIDE):
                score = lax.dot_general(
                    value, row[back, :, at], (((1,), (1,)), ((), ())),
                    preferred_element_type=jnp.float32,
                )
                score = jnp.where(col < live[back], score, -1e30)
                rowed.append(score)
                for t in range(MOSTB):
                    piece = score[:, t * 128 : (t + 1) * 128]
                    top = piece if top is None else jnp.maximum(top, piece)
            scores.append(rowed)
            highest.append(top)
        for h in range(2):
            top = jnp.broadcast_to(jnp.max(highest[h], axis=1, keepdims=True), (ROWS, 128))
            wide = jnp.concatenate([top] * MOSTB, axis=1)
            total = None
            for back in range(SIDE):
                p = jnp.exp2(scores[h][back] - wide).astype(jnp.bfloat16)
                v = jnp.where(masks[h], row[back, :, value_at], ones)
                o = jnp.dot(p, v, preferred_element_type=jnp.float32)
                total = o if total is None else total + o
            tops[d, c, h] = top
            sums[d, c, h] = total
        return carry

    lax.fori_loop(0, SIDE * (FW // 128), own_row, 0)
    for copy in [*later.values(), *query_later.values(), *sent]:
        copy.wait()


def exchange(keep_count, normed, w_qkv):
    dma = pltpu.SemaphoreType.DMA
    vmem = pl.BlockSpec(memory_space=pltpu.VMEM)
    shapes = [(SIDE, ROWS, 2 * FW)] * 3 + [(SIDE, ROWS, 2 * LW), (SIDE, ROWS, GW)]
    return pl.pallas_call(
        exchange_kernel,
        out_shape=[jax.ShapeDtypeStruct(shape, jnp.bfloat16) for shape in shapes]
        + [jax.ShapeDtypeStruct((SIDE, FW // 128, 2, ROWS, 128), jnp.float32)] * 2,
        in_specs=[pl.BlockSpec(memory_space=pltpu.SMEM), vmem, pl.BlockSpec(memory_space=pltpu.HBM)],
        out_specs=[vmem] * 7,
        scratch_shapes=[
            pltpu.VMEM((len(BLOCKS), D, GW), jnp.bfloat16),
            pltpu.VMEM((SIDE, ROWS, 2 * FW), jnp.bfloat16),
            pltpu.VMEM((SIDE, ROWS, 2 * LW), jnp.bfloat16),
            pltpu.VMEM((SIDE, ROWS, GW), jnp.bfloat16),
            dma((len(BLOCKS),)),
            *[dma((SIDE,))] * 8,
            dma((2, SIDE)),
            dma((2, SIDE)),
        ],
        compiler_params=pltpu.CompilerParams(
            collective_id=0, has_side_effects=True, vmem_limit_bytes=36 * 2**20
        ),
        name="exchange",
    )(keep_count, normed, w_qkv)


def attend_kernel(start, pairs, begun, keep, q, *refs):
    if begun:
        below, above, tops, sums = refs[:4]
        sources = ((0, below), (2, above))
    else:
        below, row, above = refs[:3]
        sources = ((0, below), (1, row), (2, above))
    out, live, keys, vals, masked, s0, s1, m0, m1, acc = refs[4 if begun else 3 :]
    y, x = place()
    for k, (dy, _) in enumerate(sources):
        for frame in range(SIDE):
            live[k * SIDE + frame] = keep[((y + SIDE - 1 + dy) % SIDE) * SIDE + frame]
    low = lax.broadcasted_iota(jnp.int32, (1, 128), 1) < HEAD_DIM
    one = jnp.ones((BLK, 128), jnp.bfloat16)
    counts = live
    total = 0
    for k, (_, kv) in enumerate(sources):

        def pack(slot, at, k=k, kv=kv):
            frame, block = slot // MOSTB, slot % MOSTB
            back = (x + SIDE - frame) % SIDE
            used = block < counts[k * SIDE + frame]

            @pl.when(used)
            def _():
                rows = pl.ds(pl.multiple_of(block * BLK, BLK), BLK)
                to = pl.ds(pl.multiple_of(at * BLK, BLK), BLK)
                for c in range(pairs):
                    keys[c, to, :] = kv[back, rows, c * 128 : (c + 1) * 128]
                    v = kv[back, rows, (pairs + c) * 128 : (pairs + c + 1) * 128]
                    vals[c, 0, to, :] = jnp.where(low, v, one)
                    vals[c, 1, to, :] = jnp.where(low, one, v)

            return at + used.astype(jnp.int32)

        total = lax.fori_loop(0, SIDE * MOSTB, pack, total)
    tail = pl.ds(pl.multiple_of(total * BLK, BLK), CH)
    for c in range(pairs):
        keys[c, tail, :] = jnp.zeros((CH, 128), jnp.bfloat16)
        for h in range(2):
            vals[c, h, tail, :] = jnp.zeros((CH, 128), jnp.bfloat16)

    def frame_rows(d, first, blocks, rows):
        full, left = blocks // (CH // BLK), blocks % (CH // BLK)
        for c in range(pairs):
            value = q[d, 0:rows, (start + c) * 128 : (start + c + 1) * 128]
            zero = jnp.zeros_like(value)
            masked[2 * c, 0:rows, :] = jnp.where(low, value, zero)
            masked[2 * c + 1, 0:rows, :] = jnp.where(low, zero, value)

        def span(j, width):
            return (
                pl.ds(pl.multiple_of(first * BLK + j * CH, BLK), width),
                pl.ds(pl.multiple_of(j * CH, BLK), width),
            )

        def score(c, j, width, partial, s, m):
            at, cols = span(j, width)
            for h in range(2):
                value = lax.dot_general(
                    masked[2 * c + h, 0:rows, :], keys[c, at, :],
                    (((1,), (1,)), ((), ())), preferred_element_type=jnp.float32,
                )
                if partial:
                    col = lax.broadcasted_iota(jnp.int32, (1, width), 1)
                    value = jnp.where(col < left * BLK, value, -1e30)
                s[h, 0:rows, cols] = value
                top = m[h, 0:rows, :]
                for t in range(width // 128):
                    top = jnp.maximum(top, value[:, t * 128 : (t + 1) * 128])
                m[h, 0:rows, :] = top

        def weigh(c, j, width, s, m):
            at, cols = span(j, width)
            for h in range(2):
                top = jnp.concatenate([m[h, 0:rows, :]] * (width // 128), axis=1)
                p = jnp.exp2(s[h, 0:rows, cols] - top).astype(jnp.bfloat16)
                acc[h, 0:rows, :] += jnp.dot(p, vals[c, h, at, :], preferred_element_type=jnp.float32)

        bufs = ((s0, m0), (s1, m1))
        for stage in range(pairs + 1):
            s, m = bufs[(stage + 1) % 2]
            sn, mn = bufs[stage % 2]
            if stage:
                top = jnp.broadcast_to(
                    jnp.max(m[:, 0:rows, :], axis=2, keepdims=True), (2, rows, 128)
                )
                if begun:
                    before = tops[d, stage - 1, :, 0:rows, :]
                    top = jnp.maximum(top, before)
                    acc[:, 0:rows, :] = sums[d, stage - 1, :, 0:rows, :] * jnp.exp2(before - top)
                else:
                    acc[:, 0:rows, :] = jnp.zeros((2, rows, 128), jnp.float32)
                m[:, 0:rows, :] = top
            if stage < pairs:
                mn[:, 0:rows, :] = jnp.full((2, rows, 128), -1e30, jnp.float32)

            def step(j, width, partial, stage=stage, s=s, m=m, sn=sn, mn=mn):
                if stage < pairs:
                    score(stage, j, width, partial, sn, mn)
                if stage:
                    weigh(stage - 1, j, width, s, m)

            lax.fori_loop(0, full, lambda j, t, step=step: (step(j, CH, False), t)[1], 0)

            @pl.when((left > 0) & (left <= CH // BLK // 2))
            def _(step=step):
                step(full, CH // 2, True)

            @pl.when(left > CH // BLK // 2)
            def _(step=step):
                step(full, CH, True)

            if stage:
                even, odd = acc[0, 0:rows, :], acc[1, 0:rows, :]
                even = even / pltpu.roll(even, HEAD_DIM, 1)
                odd = odd / pltpu.roll(odd, HEAD_DIM, 1)
                out[d, 0:rows, (stage - 1) * 128 : stage * 128] = jnp.where(low, even, odd).astype(jnp.bfloat16)

    def frame_body(f, first):
        blocks = counts[f]
        for k in range(1, len(sources) * SIDE - SIDE + 1):
            blocks += counts[f + k]
        own = keep[y * SIDE + f]
        d = (x + SIDE - f) % SIDE
        for n in range(1, MOSTB + 1):

            @pl.when(own == n)
            def _(n=n):
                frame_rows(d, first, blocks, n * BLK)
                if n < MOSTB:
                    out[d, n * BLK :, :] = jnp.zeros((ROWS - n * BLK, pairs * 128), jnp.bfloat16)

        return first + counts[f]

    lax.fori_loop(0, SIDE, frame_body, 0)


def attend(start, pairs, begun, keep_count, q, *rest):
    window = BEGUN_WINDOW if begun else WINDOW
    vmem = pl.BlockSpec(memory_space=pltpu.VMEM)
    return pl.pallas_call(
        functools.partial(attend_kernel, start, pairs, begun),
        out_shape=jax.ShapeDtypeStruct((SIDE, ROWS, pairs * 128), jnp.bfloat16),
        in_specs=[pl.BlockSpec(memory_space=pltpu.SMEM)] + [vmem] * (1 + len(rest)),
        out_specs=vmem,
        scratch_shapes=[
            pltpu.SMEM((3 * SIDE,), jnp.int32),
            pltpu.VMEM((pairs, KROWS, 128), jnp.bfloat16),
            pltpu.VMEM((pairs, 2, KROWS, 128), jnp.bfloat16),
            pltpu.VMEM((2 * pairs, ROWS, 128), jnp.bfloat16),
            pltpu.VMEM((2, ROWS, window), jnp.float32),
            pltpu.VMEM((2, ROWS, window), jnp.float32),
            *[pltpu.VMEM((2, ROWS, 128), jnp.float32)] * 3,
        ],
        compiler_params=pltpu.CompilerParams(vmem_limit_bytes=(32 if begun else 36) * 2**20),
        cost_estimate=pl.CostEstimate(
            flops=pairs * 18 * 10**9, bytes_accessed=pairs * 2**21, transcendentals=0
        ),
        name="attend",
    )(keep_count, q, *rest)


def project_kernel(own, one, two, three, rest, w, out, got, wbuf, total, wsem, ss, rs):
    y, x = place()
    order = (0, 1, 3, 2)
    loads = []
    for i, delta in enumerate(order):
        row = pl.multiple_of(((x - delta) % SIDE) * GW, GW)
        load = pltpu.make_async_copy(w.at[pl.ds(row, GW), :], wbuf.at[i], wsem.at[i])
        load.start()
        loads.append(load)
    barrier = pltpu.get_barrier_semaphore()
    for delta in (1, 2, 3):
        pl.semaphore_signal(barrier, inc=1, device_id=device(y, x + delta), device_id_type=MESH)
    pl.semaphore_wait(barrier, 3)
    copies = {}
    for delta in (2, 1, 3):
        copies[delta] = pltpu.make_async_remote_copy(
            rest.at[(SIDE - delta) % SIDE], got.at[delta], ss.at[delta], rs.at[delta],
            device_id=device(y, x + delta), device_id_type=MESH,
        )
        copies[delta].start()
    parts = (own, one, two, three)
    for i, delta in enumerate(order):
        loads[i].wait()

        def first(r, carry, i=i, delta=delta):
            at = pl.ds(pl.multiple_of(r * BLK, BLK), BLK)
            value = jnp.dot(parts[delta][at, :], wbuf[i, :FW, :], preferred_element_type=jnp.float32)
            if i == 0:
                value += jnp.dot(rest[0, at, :], wbuf[i, FW:, :], preferred_element_type=jnp.float32)
            else:
                value += total[at, :]
            total[at, :] = value
            return carry

        lax.fori_loop(0, MOSTB, first, 0)
    for i, delta in enumerate(order):
        if delta == 0:
            continue
        copies[delta].wait()

        def rows(r, carry, i=i, delta=delta):
            at = pl.ds(pl.multiple_of(r * BLK, BLK), BLK)
            value = total[at, :]
            value += jnp.dot(got[delta, at, :], wbuf[i, FW:, :], preferred_element_type=jnp.float32)
            if i < SIDE - 1:
                total[at, :] = value
            else:
                scale = lax.rsqrt(jnp.mean(value * value, axis=-1, keepdims=True) + 1e-06)
                out[at, :] = (value * scale).astype(jnp.bfloat16)
            return carry

        lax.fori_loop(0, MOSTB, rows, 0)


def project(parts, rest, w_out):
    dma = pltpu.SemaphoreType.DMA
    vmem = pl.BlockSpec(memory_space=pltpu.VMEM)
    return pl.pallas_call(
        project_kernel,
        out_shape=jax.ShapeDtypeStruct((ROWS, D), jnp.bfloat16),
        in_specs=[vmem] * 5 + [pl.BlockSpec(memory_space=pltpu.HBM)],
        out_specs=vmem,
        scratch_shapes=[
            pltpu.VMEM((SIDE, ROWS, LW), jnp.bfloat16),
            pltpu.VMEM((SIDE, GW, D), jnp.bfloat16),
            pltpu.VMEM((ROWS, D), jnp.float32),
            *[dma((SIDE,))] * 3,
        ],
        compiler_params=pltpu.CompilerParams(
            collective_id=1, has_side_effects=True, vmem_limit_bytes=24 * 2**20
        ),
        name="project",
    )(*parts, rest, w_out)


def scatter_kernel(order, count, block, out, zero, sems):
    own = count[lax.axis_index("frame")]
    zero[...] = jnp.zeros_like(zero)

    def each(act):
        for j in range(order.shape[1]):
            rows = pl.ds(pl.multiple_of(order[0, j] * BLK, BLK), BLK)
            if j == MOSTB:
                act(pltpu.make_async_copy(zero, out.at[rows, :], sems.at[j]))
                continue

            @pl.when(j < own)
            def _(j=j, rows=rows):
                act(pltpu.make_async_copy(block.at[pl.ds(j * BLK, BLK), :], out.at[rows, :], sems.at[j]))

            @pl.when(j >= own)
            def _(j=j, rows=rows):
                act(pltpu.make_async_copy(zero, out.at[rows, :], sems.at[j]))

    each(lambda copy: copy.start())
    each(lambda copy: copy.wait())


def scatter(keep_order, keep_count, normalized):
    blocks = keep_order.shape[1]
    smem = pl.BlockSpec(memory_space=pltpu.SMEM)
    return pl.pallas_call(
        scatter_kernel,
        in_specs=[smem, smem, pl.BlockSpec(memory_space=pltpu.VMEM)],
        out_specs=pl.BlockSpec(memory_space=pl.ANY),
        out_shape=jax.ShapeDtypeStruct((blocks * BLK, D), jnp.bfloat16),
        scratch_shapes=[pltpu.VMEM((BLK, D), jnp.bfloat16), pltpu.SemaphoreType.DMA((blocks,))],
        compiler_params=pltpu.CompilerParams(vmem_limit_bytes=8 * 2**20),
        name="scatter",
    )(keep_order, keep_count, normalized)


def shifted(value, dy, dx):
    def to(f):
        return (f // SIDE + dy) % SIDE * SIDE + (f + dx) % SIDE

    return lax.ppermute(value, "frame", [(f, to(f)) for f in range(SIDE * SIDE)])


def shards(tokens, keep_count, keep_order, w_qkv, w_out):
    normed = norm_kept(keep_order, tokens)
    below, row, above, last, q, tops, sums = exchange(keep_count, normed, w_qkv)
    last_below = shifted(last, 1, 0)
    last_above = shifted(last, -1, 0)
    part = attend(0, 2, True, keep_count, q, below, above, tops, sums)
    parts = [shifted(part[(SIDE - dx) % SIDE], 0, dx) if dx else part[0] for dx in range(SIDE)]
    rest = attend(2, 1, False, keep_count, q, last_below, last, last_above)
    normalized = project(parts, rest, w_out)
    return scatter(keep_order, keep_count, normalized)


def solution(mesh):
    return jax.shard_map(
        shards,
        mesh=mesh,
        in_specs=(P(("orbit", "frame"), None), P("orbit"), P(("orbit", "frame"), None), P(), P()),
        out_specs=P(("orbit", "frame"), None),
        check_vma=False,
    )
```

```python
import functools

import jax
import jax.numpy as jnp
from jax import lax
from jax.experimental import pallas as pl
from jax.experimental.pallas import tpu as pltpu
from jax.sharding import PartitionSpec as P

D = 1536
HEADS = 24
HEAD_DIM = 64
BLK = 128
MOSTB = 3
ROWS = MOSTB * BLK
SIDE = 4
GW = 384
CH = 1024
WINDOW = 28 * BLK
BEGUN_WINDOW = 16 * BLK
KROWS = 36 * BLK + CH
SCALE = HEAD_DIM ** (-0.5) * 1.4426950408889634
MESH = pl.DeviceIdType.MESH


def place():
    me = lax.axis_index("frame")
    return me // SIDE, me % SIDE


def device(y, x):
    return {"frame": (y % SIDE) * SIDE + x % SIDE}


def norm_kernel(order, tokens, out, kept, sems):
    loads = []
    for j in range(MOSTB):
        rows = pl.ds(pl.multiple_of(order[0, j] * BLK, BLK), BLK)
        loads.append(pltpu.make_async_copy(tokens.at[rows, :], kept.at[j], sems.at[j]))
        loads[j].start()
    for j in range(MOSTB):
        loads[j].wait()
        wide = kept[j].astype(jnp.float32)
        scale = lax.rsqrt(jnp.mean(wide * wide, axis=-1, keepdims=True) + 1e-06)
        out[j * BLK : (j + 1) * BLK, :] = (wide * scale).astype(jnp.bfloat16)


def norm_kept(keep_order, tokens):
    return pl.pallas_call(
        norm_kernel,
        in_specs=[pl.BlockSpec(memory_space=pltpu.SMEM), pl.BlockSpec(memory_space=pltpu.HBM)],
        out_specs=pl.BlockSpec(memory_space=pltpu.VMEM),
        out_shape=jax.ShapeDtypeStruct((ROWS, D), jnp.bfloat16),
        scratch_shapes=[pltpu.VMEM((MOSTB, BLK, D), jnp.bfloat16), pltpu.SemaphoreType.DMA((MOSTB,))],
        compiler_params=pltpu.CompilerParams(vmem_limit_bytes=12 * 2**20),
        name="norm_kept",
    )(keep_order, tokens)


BLOCKS = ((1, 1), (1, 2), (0, 1), (0, 2), (3, 1), (3, 2), (2, 1), (2, 2), (1, 0), (3, 0), (2, 0), (0, 0))
FW = 256
LW = GW - FW


def exchange_kernel(
    keep, normed, w, below, row, above, last, q, tops, sums, wbuf, kvs, lasts, qs,
    wsem, xs, xr, ls, lr, qss, qsr, rss, rsr, ys, yr,
):
    y, x = place()
    loads = []
    for i, (delta, kind) in enumerate(BLOCKS):
        col = pl.multiple_of(kind * (HEADS * HEAD_DIM) + ((x + delta) % SIDE) * GW, 128)
        load = pltpu.make_async_copy(w.at[:, pl.ds(col, GW)], wbuf.at[i], wsem.at[i])
        load.start()
        loads.append(load)
    barrier = pltpu.get_barrier_semaphore()
    peers = [(0, 1), (0, 2), (0, 3), (1, 0), (3, 0)]
    for dy, dx in peers:
        pl.semaphore_signal(barrier, inc=1, device_id=device(y + dy, x + dx), device_id_type=MESH)

    def product(i, put):
        loads[i].wait()

        def rows(r, carry):
            at = pl.ds(pl.multiple_of(r * BLK, BLK), BLK)
            value = jnp.dot(normed[at, :], wbuf[i], preferred_element_type=jnp.float32)
            put(at, value)
            return carry

        lax.fori_loop(0, MOSTB, rows, 0)

    def across(src, dst, send, recv, delta):
        return pltpu.make_async_remote_copy(
            src.at[delta], dst.at[delta], send.at[delta], recv.at[delta],
            device_id=device(y, x + delta), device_id_type=MESH,
        )

    first = {delta: across(kvs, row, xs, xr, delta) for delta in (1, 2, 3)}
    later = {delta: across(lasts, last, ls, lr, delta) for delta in (1, 2, 3)}
    part, rest = (slice(None), slice(None), pl.ds(0, FW)), (slice(None), slice(None), pl.ds(FW, LW))
    query = {delta: across(qs.at[part], q.at[part], qss, qsr, delta) for delta in (1, 2, 3)}
    query_later = {delta: across(qs.at[rest], q.at[rest], rss, rsr, delta) for delta in (1, 2, 3)}
    sent = []

    def up_down(delta):
        for way, (dy, to) in enumerate(((1, below), (-1, above))):
            copy = pltpu.make_async_remote_copy(
                row.at[delta], to.at[delta], ys.at[way, delta], yr.at[way, delta],
                device_id=device(y + dy, x), device_id_type=MESH,
            )
            copy.start()
            sent.append(copy)

    for i, (delta, kind) in enumerate(BLOCKS):
        if kind == 0:
            to = q if delta == 0 else qs

            def put(at, value, delta=delta, to=to):
                to[delta, at, :] = (value * SCALE).astype(jnp.bfloat16)
        else:
            to, rest = (row, last) if delta == 0 else (kvs, lasts)

            def put(at, value, delta=delta, kind=kind, to=to, rest=rest):
                value = value.astype(jnp.bfloat16)
                to[delta, at, pl.ds((kind - 1) * FW, FW)] = value[:, :FW]
                rest[delta, at, pl.ds((kind - 1) * LW, LW)] = value[:, FW:]

        product(i, put)
        if i == 1:
            pl.semaphore_wait(barrier, len(peers))
        if kind == 2:
            if delta == 0:
                up_down(0)
            else:
                first[delta].start()
    first[1].wait()
    up_down(1)
    first[3].wait()
    up_down(3)
    for delta in (1, 3, 2):
        query[delta].start()
    first[2].wait()
    up_down(2)
    for delta in (1, 3, 2):
        later[delta].start()
    for delta in (1, 3, 2):
        query_later[delta].start()
    live = [keep[y * SIDE + (x + SIDE - back) % SIDE] * BLK for back in range(SIDE)]
    low = lax.broadcasted_iota(jnp.int32, (1, 128), 1) < HEAD_DIM
    col = lax.broadcasted_iota(jnp.int32, (1, ROWS), 1)
    ones = jnp.ones((ROWS, 128), jnp.bfloat16)

    def own_row(i, carry):
        d, c = i // (FW // 128), i % (FW // 128)

        @pl.when((d > 0) & (c == 0))
        def _():
            across(qs.at[part], q.at[part], qss, qsr, d).wait()

        at = pl.ds(pl.multiple_of(c * 128, 128), 128)
        value_at = pl.ds(pl.multiple_of(FW + c * 128, 128), 128)
        masks = (low, jnp.logical_not(low))
        query_pair = q[d, :, at]
        scores, highest = [], []
        for h in range(2):
            value = jnp.where(masks[h], query_pair, jnp.zeros_like(query_pair))
            rowed = []
            top = None
            for back in range(SIDE):
                score = lax.dot_general(
                    value, row[back, :, at], (((1,), (1,)), ((), ())),
                    preferred_element_type=jnp.float32,
                )
                score = jnp.where(col < live[back], score, -1e30)
                rowed.append(score)
                for t in range(MOSTB):
                    piece = score[:, t * 128 : (t + 1) * 128]
                    top = piece if top is None else jnp.maximum(top, piece)
            scores.append(rowed)
            highest.append(top)
        for h in range(2):
            top = jnp.broadcast_to(jnp.max(highest[h], axis=1, keepdims=True), (ROWS, 128))
            wide = jnp.concatenate([top] * MOSTB, axis=1)
            total = None
            for back in range(SIDE):
                p = jnp.exp2(scores[h][back] - wide).astype(jnp.bfloat16)
                v = jnp.where(masks[h], row[back, :, value_at], ones)
                o = jnp.dot(p, v, preferred_element_type=jnp.float32)
                total = o if total is None else total + o
            tops[d, c, h] = top
            sums[d, c, h] = total
        return carry

    lax.fori_loop(0, SIDE * (FW // 128), own_row, 0)
    for copy in [*later.values(), *query_later.values(), *sent]:
        copy.wait()


def exchange(keep_count, normed, w_qkv):
    dma = pltpu.SemaphoreType.DMA
    vmem = pl.BlockSpec(memory_space=pltpu.VMEM)
    shapes = [(SIDE, ROWS, 2 * FW)] * 3 + [(SIDE, ROWS, 2 * LW), (SIDE, ROWS, GW)]
    return pl.pallas_call(
        exchange_kernel,
        out_shape=[jax.ShapeDtypeStruct(shape, jnp.bfloat16) for shape in shapes]
        + [jax.ShapeDtypeStruct((SIDE, FW // 128, 2, ROWS, 128), jnp.float32)] * 2,
        in_specs=[pl.BlockSpec(memory_space=pltpu.SMEM), vmem, pl.BlockSpec(memory_space=pltpu.HBM)],
        out_specs=[vmem] * 7,
        scratch_shapes=[
            pltpu.VMEM((len(BLOCKS), D, GW), jnp.bfloat16),
            pltpu.VMEM((SIDE, ROWS, 2 * FW), jnp.bfloat16),
            pltpu.VMEM((SIDE, ROWS, 2 * LW), jnp.bfloat16),
            pltpu.VMEM((SIDE, ROWS, GW), jnp.bfloat16),
            dma((len(BLOCKS),)),
            *[dma((SIDE,))] * 8,
            dma((2, SIDE)),
            dma((2, SIDE)),
        ],
        compiler_params=pltpu.CompilerParams(
            collective_id=0, has_side_effects=True, vmem_limit_bytes=36 * 2**20
        ),
        name="exchange",
    )(keep_count, normed, w_qkv)


def attend_kernel(start, pairs, begun, keep, q, *refs):
    if begun:
        below, above, tops, sums = refs[:4]
        sources = ((0, below), (2, above))
    else:
        below, row, above = refs[:3]
        sources = ((0, below), (1, row), (2, above))
    out, live, keys, vals, masked, s0, s1, m0, m1, acc = refs[4 if begun else 3 :]
    y, x = place()
    for k, (dy, _) in enumerate(sources):
        for frame in range(SIDE):
            live[k * SIDE + frame] = keep[((y + SIDE - 1 + dy) % SIDE) * SIDE + frame]
    low = lax.broadcasted_iota(jnp.int32, (1, 128), 1) < HEAD_DIM
    one = jnp.ones((BLK, 128), jnp.bfloat16)
    counts = live
    total = 0
    for k, (_, kv) in enumerate(sources):

        def pack(slot, at, k=k, kv=kv):
            frame, block = slot // MOSTB, slot % MOSTB
            back = (x + SIDE - frame) % SIDE
            used = block < counts[k * SIDE + frame]

            @pl.when(used)
            def _():
                rows = pl.ds(pl.multiple_of(block * BLK, BLK), BLK)
                to = pl.ds(pl.multiple_of(at * BLK, BLK), BLK)
                for c in range(pairs):
                    keys[c, to, :] = kv[back, rows, c * 128 : (c + 1) * 128]
                    v = kv[back, rows, (pairs + c) * 128 : (pairs + c + 1) * 128]
                    vals[c, 0, to, :] = jnp.where(low, v, one)
                    vals[c, 1, to, :] = jnp.where(low, one, v)

            return at + used.astype(jnp.int32)

        total = lax.fori_loop(0, SIDE * MOSTB, pack, total)
    tail = pl.ds(pl.multiple_of(total * BLK, BLK), CH)
    for c in range(pairs):
        keys[c, tail, :] = jnp.zeros((CH, 128), jnp.bfloat16)
        for h in range(2):
            vals[c, h, tail, :] = jnp.zeros((CH, 128), jnp.bfloat16)

    def frame_rows(d, first, blocks, rows):
        full, left = blocks // (CH // BLK), blocks % (CH // BLK)
        for c in range(pairs):
            value = q[d, 0:rows, (start + c) * 128 : (start + c + 1) * 128]
            zero = jnp.zeros_like(value)
            masked[2 * c, 0:rows, :] = jnp.where(low, value, zero)
            masked[2 * c + 1, 0:rows, :] = jnp.where(low, zero, value)

        def span(j, width):
            return (
                pl.ds(pl.multiple_of(first * BLK + j * CH, BLK), width),
                pl.ds(pl.multiple_of(j * CH, BLK), width),
            )

        def score(c, j, width, partial, s, m):
            at, cols = span(j, width)
            for h in range(2):
                value = lax.dot_general(
                    masked[2 * c + h, 0:rows, :], keys[c, at, :],
                    (((1,), (1,)), ((), ())), preferred_element_type=jnp.float32,
                )
                if partial:
                    col = lax.broadcasted_iota(jnp.int32, (1, width), 1)
                    value = jnp.where(col < left * BLK, value, -1e30)
                s[h, 0:rows, cols] = value
                top = m[h, 0:rows, :]
                for t in range(width // 128):
                    top = jnp.maximum(top, value[:, t * 128 : (t + 1) * 128])
                m[h, 0:rows, :] = top

        def weigh(c, j, width, s, m):
            at, cols = span(j, width)
            for h in range(2):
                top = jnp.concatenate([m[h, 0:rows, :]] * (width // 128), axis=1)
                p = jnp.exp2(s[h, 0:rows, cols] - top).astype(jnp.bfloat16)
                acc[h, 0:rows, :] += jnp.dot(p, vals[c, h, at, :], preferred_element_type=jnp.float32)

        bufs = ((s0, m0), (s1, m1))
        for stage in range(pairs + 1):
            s, m = bufs[(stage + 1) % 2]
            sn, mn = bufs[stage % 2]
            if stage:
                top = jnp.broadcast_to(
                    jnp.max(m[:, 0:rows, :], axis=2, keepdims=True), (2, rows, 128)
                )
                if begun:
                    before = tops[d, stage - 1, :, 0:rows, :]
                    top = jnp.maximum(top, before)
                    acc[:, 0:rows, :] = sums[d, stage - 1, :, 0:rows, :] * jnp.exp2(before - top)
                else:
                    acc[:, 0:rows, :] = jnp.zeros((2, rows, 128), jnp.float32)
                m[:, 0:rows, :] = top
            if stage < pairs:
                mn[:, 0:rows, :] = jnp.full((2, rows, 128), -1e30, jnp.float32)

            def step(j, width, partial, stage=stage, s=s, m=m, sn=sn, mn=mn):
                if stage < pairs:
                    score(stage, j, width, partial, sn, mn)
                if stage:
                    weigh(stage - 1, j, width, s, m)

            lax.fori_loop(0, full, lambda j, t, step=step: (step(j, CH, False), t)[1], 0)

            @pl.when((left > 0) & (left <= CH // BLK // 2))
            def _(step=step):
                step(full, CH // 2, True)

            @pl.when(left > CH // BLK // 2)
            def _(step=step):
                step(full, CH, True)

            if stage:
                even, odd = acc[0, 0:rows, :], acc[1, 0:rows, :]
                even = even / pltpu.roll(even, HEAD_DIM, 1)
                odd = odd / pltpu.roll(odd, HEAD_DIM, 1)
                out[d, 0:rows, (stage - 1) * 128 : stage * 128] = jnp.where(low, even, odd).astype(jnp.bfloat16)

    def frame_body(f, first):
        blocks = counts[f]
        for k in range(1, len(sources) * SIDE - SIDE + 1):
            blocks += counts[f + k]
        own = keep[y * SIDE + f]
        d = (x + SIDE - f) % SIDE
        for n in range(1, MOSTB + 1):

            @pl.when(own == n)
            def _(n=n):
                frame_rows(d, first, blocks, n * BLK)
                if n < MOSTB:
                    out[d, n * BLK :, :] = jnp.zeros((ROWS - n * BLK, pairs * 128), jnp.bfloat16)

        return first + counts[f]

    lax.fori_loop(0, SIDE, frame_body, 0)


def attend(start, pairs, begun, keep_count, q, *rest):
    window = BEGUN_WINDOW if begun else WINDOW
    vmem = pl.BlockSpec(memory_space=pltpu.VMEM)
    return pl.pallas_call(
        functools.partial(attend_kernel, start, pairs, begun),
        out_shape=jax.ShapeDtypeStruct((SIDE, ROWS, pairs * 128), jnp.bfloat16),
        in_specs=[pl.BlockSpec(memory_space=pltpu.SMEM)] + [vmem] * (1 + len(rest)),
        out_specs=vmem,
        scratch_shapes=[
            pltpu.SMEM((3 * SIDE,), jnp.int32),
            pltpu.VMEM((pairs, KROWS, 128), jnp.bfloat16),
            pltpu.VMEM((pairs, 2, KROWS, 128), jnp.bfloat16),
            pltpu.VMEM((2 * pairs, ROWS, 128), jnp.bfloat16),
            pltpu.VMEM((2, ROWS, window), jnp.float32),
            pltpu.VMEM((2, ROWS, window), jnp.float32),
            *[pltpu.VMEM((2, ROWS, 128), jnp.float32)] * 3,
        ],
        compiler_params=pltpu.CompilerParams(vmem_limit_bytes=(32 if begun else 36) * 2**20),
        cost_estimate=pl.CostEstimate(
            flops=pairs * 18 * 10**9, bytes_accessed=pairs * 2**21, transcendentals=0
        ),
        name="attend",
    )(keep_count, q, *rest)


def project_kernel(own, one, two, three, rest, w, out, got, most, few, total, wsem, ss, rs):
    y, x = place()
    barrier = pltpu.get_barrier_semaphore()
    for delta in (1, 2, 3):
        pl.semaphore_signal(barrier, inc=1, device_id=device(y, x + delta), device_id_type=MESH)
    loads = []
    for delta in range(SIDE):
        group = ((x + SIDE - delta) % SIDE) * GW
        for k, (skip, size, to) in enumerate(((0, FW, most), (FW, LW, few))):
            rows = pl.ds(pl.multiple_of(group + skip, LW), size)
            load = pltpu.make_async_copy(w.at[rows, :], to.at[pl.ds(delta * size, size), :], wsem.at[k, delta])
            load.start()
            loads.append(load)
    pl.semaphore_wait(barrier, 3)
    copies = []
    for delta in (2, 1, 3):
        copy = pltpu.make_async_remote_copy(
            rest.at[(SIDE - delta) % SIDE], got.at[delta], ss.at[delta], rs.at[delta],
            device_id=device(y, x + delta), device_id_type=MESH,
        )
        copy.start()
        copies.append(copy)
    for load in loads:
        load.wait()
    tile = 512

    def first(t, carry):
        cols = pl.ds(pl.multiple_of(t * tile, 128), tile)
        left = jnp.concatenate([own[...], one[...], two[...], three[...], rest[0]], axis=1)
        right = jnp.concatenate([most[:, cols], few[0:LW, cols]], axis=0)
        total[:, cols] = jnp.dot(left, right, preferred_element_type=jnp.float32)
        return carry

    lax.fori_loop(0, D // tile, first, 0)
    for copy in copies:
        copy.wait()

    def second(t, square):
        cols = pl.ds(pl.multiple_of(t * tile, 128), tile)
        left = jnp.concatenate([got[1], got[2], got[3]], axis=1)
        value = total[:, cols] + jnp.dot(left, few[LW:, cols], preferred_element_type=jnp.float32)
        total[:, cols] = value
        for k in range(tile // 128):
            piece = value[:, k * 128 : (k + 1) * 128]
            square += piece * piece
        return square

    square = lax.fori_loop(0, D // tile, second, jnp.zeros((ROWS, 128), jnp.float32))
    scale = lax.rsqrt(jnp.sum(square, axis=1, keepdims=True) / D + 1e-06)
    scale = jnp.broadcast_to(scale, (ROWS, 128))
    for k in range(D // 128):
        cols = slice(k * 128, (k + 1) * 128)
        out[:, cols] = (total[:, cols] * scale).astype(jnp.bfloat16)


def project(parts, rest, w_out):
    dma = pltpu.SemaphoreType.DMA
    vmem = pl.BlockSpec(memory_space=pltpu.VMEM)
    return pl.pallas_call(
        project_kernel,
        out_shape=jax.ShapeDtypeStruct((ROWS, D), jnp.bfloat16),
        in_specs=[vmem] * 5 + [pl.BlockSpec(memory_space=pltpu.HBM)],
        out_specs=vmem,
        scratch_shapes=[
            pltpu.VMEM((SIDE, ROWS, LW), jnp.bfloat16),
            pltpu.VMEM((SIDE * FW, D), jnp.bfloat16),
            pltpu.VMEM((SIDE * LW, D), jnp.bfloat16),
            pltpu.VMEM((ROWS, D), jnp.float32),
            dma((2, SIDE)),
            dma((SIDE,)),
            dma((SIDE,)),
        ],
        compiler_params=pltpu.CompilerParams(
            collective_id=1, has_side_effects=True, vmem_limit_bytes=24 * 2**20
        ),
        name="project",
    )(*parts, rest, w_out)


def scatter_kernel(order, count, block, out, zero, sems):
    own = count[lax.axis_index("frame")]
    zero[...] = jnp.zeros_like(zero)

    def each(act):
        for j in range(order.shape[1]):
            rows = pl.ds(pl.multiple_of(order[0, j] * BLK, BLK), BLK)
            if j == MOSTB:
                act(pltpu.make_async_copy(zero, out.at[rows, :], sems.at[j]))
                continue

            @pl.when(j < own)
            def _(j=j, rows=rows):
                act(pltpu.make_async_copy(block.at[pl.ds(j * BLK, BLK), :], out.at[rows, :], sems.at[j]))

            @pl.when(j >= own)
            def _(j=j, rows=rows):
                act(pltpu.make_async_copy(zero, out.at[rows, :], sems.at[j]))

    each(lambda copy: copy.start())
    each(lambda copy: copy.wait())


def scatter(keep_order, keep_count, normalized):
    blocks = keep_order.shape[1]
    smem = pl.BlockSpec(memory_space=pltpu.SMEM)
    return pl.pallas_call(
        scatter_kernel,
        in_specs=[smem, smem, pl.BlockSpec(memory_space=pltpu.VMEM)],
        out_specs=pl.BlockSpec(memory_space=pl.ANY),
        out_shape=jax.ShapeDtypeStruct((blocks * BLK, D), jnp.bfloat16),
        scratch_shapes=[pltpu.VMEM((BLK, D), jnp.bfloat16), pltpu.SemaphoreType.DMA((blocks,))],
        compiler_params=pltpu.CompilerParams(vmem_limit_bytes=8 * 2**20),
        name="scatter",
    )(keep_order, keep_count, normalized)


def shifted(value, dy, dx):
    def to(f):
        return (f // SIDE + dy) % SIDE * SIDE + (f + dx) % SIDE

    return lax.ppermute(value, "frame", [(f, to(f)) for f in range(SIDE * SIDE)])


def shards(tokens, keep_count, keep_order, w_qkv, w_out):
    normed = norm_kept(keep_order, tokens)
    below, row, above, last, q, tops, sums = exchange(keep_count, normed, w_qkv)
    last_below = shifted(last, 1, 0)
    last_above = shifted(last, -1, 0)
    part = attend(0, 2, True, keep_count, q, below, above, tops, sums)
    parts = [shifted(part[(SIDE - dx) % SIDE], 0, dx) if dx else part[0] for dx in range(SIDE)]
    rest = attend(2, 1, False, keep_count, q, last_below, last, last_above)
    normalized = project(parts, rest, w_out)
    return scatter(keep_order, keep_count, normalized)


def solution(mesh):
    return jax.shard_map(
        shards,
        mesh=mesh,
        in_specs=(P(("orbit", "frame"), None), P("orbit"), P(("orbit", "frame"), None), P(), P()),
        out_specs=P(("orbit", "frame"), None),
        check_vma=False,
    )
```

```python
import functools

import jax
import jax.numpy as jnp
from jax import lax
from jax.experimental import pallas as pl
from jax.experimental.pallas import tpu as pltpu
from jax.sharding import PartitionSpec as P

D = 1536
HEADS = 24
HEAD_DIM = 64
BLK = 128
MOSTB = 3
ROWS = MOSTB * BLK
SIDE = 4
GW = 384
CH = 1024
WINDOW = 28 * BLK
BEGUN_WINDOW = 16 * BLK
KROWS = 36 * BLK + CH
SCALE = HEAD_DIM ** (-0.5) * 1.4426950408889634
MESH = pl.DeviceIdType.MESH


def place():
    me = lax.axis_index("frame")
    return me // SIDE, me % SIDE


def device(y, x):
    return {"frame": (y % SIDE) * SIDE + x % SIDE}


def norm_kernel(order, tokens, out):
    for j in range(MOSTB):
        rows = pl.ds(pl.multiple_of(order[0, j] * BLK, BLK), BLK)
        wide = tokens[rows, :].astype(jnp.float32)
        scale = lax.rsqrt(jnp.mean(wide * wide, axis=-1, keepdims=True) + 1e-06)
        out[j * BLK : (j + 1) * BLK, :] = (wide * scale).astype(jnp.bfloat16)


def norm_kept(keep_order, tokens):
    vmem = pl.BlockSpec(memory_space=pltpu.VMEM)
    return pl.pallas_call(
        norm_kernel,
        in_specs=[pl.BlockSpec(memory_space=pltpu.SMEM), vmem],
        out_specs=vmem,
        out_shape=jax.ShapeDtypeStruct((ROWS, D), jnp.bfloat16),
        compiler_params=pltpu.CompilerParams(vmem_limit_bytes=12 * 2**20),
        name="norm_kept",
    )(keep_order, tokens)


BLOCKS = ((1, 1), (1, 2), (0, 1), (0, 2), (3, 1), (3, 2), (2, 1), (2, 2), (1, 0), (3, 0), (2, 0), (0, 0))
FW = 256
LW = GW - FW


def exchange_kernel(
    keep, normed, w, below, row, above, mine_below, mine, mine_above, last, q, tops, sums,
    wbuf, kvs, lasts, qs, wsem, xs, xr, ls, lr, qss, qsr, rss, rsr, ys, yr, ms, mr,
):
    y, x = place()
    loads = []
    for i, (delta, kind) in enumerate(BLOCKS):
        col = pl.multiple_of(kind * (HEADS * HEAD_DIM) + ((x + delta) % SIDE) * GW, 128)
        load = pltpu.make_async_copy(w.at[:, pl.ds(col, GW)], wbuf.at[i], wsem.at[i])
        load.start()
        loads.append(load)
    barrier = pltpu.get_barrier_semaphore()
    peers = [(0, 1), (0, 2), (0, 3), (1, 0), (3, 0)]
    for dy, dx in peers:
        pl.semaphore_signal(barrier, inc=1, device_id=device(y + dy, x + dx), device_id_type=MESH)

    def product(i, put):
        loads[i].wait()

        def rows(r, carry):
            at = pl.ds(pl.multiple_of(r * BLK, BLK), BLK)
            value = jnp.dot(normed[at, :], wbuf[i], preferred_element_type=jnp.float32)
            put(at, value)
            return carry

        lax.fori_loop(0, MOSTB, rows, 0)

    def across(src, dst, send, recv, delta):
        return pltpu.make_async_remote_copy(
            src.at[delta], dst.at[delta], send.at[delta], recv.at[delta],
            device_id=device(y, x + delta), device_id_type=MESH,
        )

    first = {delta: across(kvs, row, xs, xr, delta) for delta in (1, 2, 3)}
    later = {
        delta: pltpu.make_async_remote_copy(
            lasts.at[delta], last.at[delta - 1], ls.at[delta], lr.at[delta],
            device_id=device(y, x + delta), device_id_type=MESH,
        )
        for delta in (1, 2, 3)
    }
    part, rest = (slice(None), slice(None), pl.ds(0, FW)), (slice(None), slice(None), pl.ds(FW, LW))
    query = {delta: across(qs.at[part], q.at[part], qss, qsr, delta) for delta in (1, 2, 3)}
    query_later = {delta: across(qs.at[rest], q.at[rest], rss, rsr, delta) for delta in (1, 2, 3)}
    sent = []

    def up_down(delta):
        for way, (dy, to) in enumerate(((1, below), (-1, above))):
            copy = pltpu.make_async_remote_copy(
                row.at[delta], to.at[delta], ys.at[way, delta], yr.at[way, delta],
                device_id=device(y + dy, x), device_id_type=MESH,
            )
            copy.start()
            sent.append(copy)

    for i, (delta, kind) in enumerate(BLOCKS):
        if kind == 0:
            to = q if delta == 0 else qs

            def put(at, value, delta=delta, to=to):
                to[delta, at, :] = (value * SCALE).astype(jnp.bfloat16)
        else:
            to, rest = (row, mine) if delta == 0 else (kvs, lasts)

            def put(at, value, delta=delta, kind=kind, to=to, rest=rest):
                value = value.astype(jnp.bfloat16)
                to[delta, at, pl.ds((kind - 1) * FW, FW)] = value[:, :FW]
                rest[delta, at, pl.ds((kind - 1) * LW, LW)] = value[:, FW:]

        product(i, put)
        if i == 1:
            pl.semaphore_wait(barrier, len(peers))
        if kind == 2:
            if delta == 0:
                up_down(0)
                for way, (dy, to) in enumerate(((1, mine_below), (-1, mine_above))):
                    copy = pltpu.make_async_remote_copy(
                        mine, to, ms.at[way], mr.at[way],
                        device_id=device(y + dy, x), device_id_type=MESH,
                    )
                    copy.start()
                    sent.append(copy)
            else:
                first[delta].start()
    first[1].wait()
    up_down(1)
    first[3].wait()
    up_down(3)
    for delta in (1, 3, 2):
        query[delta].start()
    first[2].wait()
    up_down(2)
    for delta in (1, 3, 2):
        later[delta].start()
    for delta in (1, 3, 2):
        query_later[delta].start()
    live = [keep[y * SIDE + (x + SIDE - back) % SIDE] * BLK for back in range(SIDE)]
    low = lax.broadcasted_iota(jnp.int32, (1, 128), 1) < HEAD_DIM
    col = lax.broadcasted_iota(jnp.int32, (1, ROWS), 1)
    ones = jnp.ones((ROWS, 128), jnp.bfloat16)

    def own_row(i, carry):
        d, c = i // (FW // 128), i % (FW // 128)

        @pl.when((d > 0) & (c == 0))
        def _():
            across(qs.at[part], q.at[part], qss, qsr, d).wait()

        at = pl.ds(pl.multiple_of(c * 128, 128), 128)
        value_at = pl.ds(pl.multiple_of(FW + c * 128, 128), 128)
        masks = (low, jnp.logical_not(low))
        query_pair = q[d, :, at]
        scores, highest = [], []
        for h in range(2):
            value = jnp.where(masks[h], query_pair, jnp.zeros_like(query_pair))
            rowed = []
            top = None
            for back in range(SIDE):
                score = lax.dot_general(
                    value, row[back, :, at], (((1,), (1,)), ((), ())),
                    preferred_element_type=jnp.float32,
                )
                score = jnp.where(col < live[back], score, -1e30)
                rowed.append(score)
                for t in range(MOSTB):
                    piece = score[:, t * 128 : (t + 1) * 128]
                    top = piece if top is None else jnp.maximum(top, piece)
            scores.append(rowed)
            highest.append(top)
        for h in range(2):
            top = jnp.broadcast_to(jnp.max(highest[h], axis=1, keepdims=True), (ROWS, 128))
            wide = jnp.concatenate([top] * MOSTB, axis=1)
            total = None
            for back in range(SIDE):
                p = jnp.exp2(scores[h][back] - wide).astype(jnp.bfloat16)
                v = jnp.where(masks[h], row[back, :, value_at], ones)
                o = jnp.dot(p, v, preferred_element_type=jnp.float32)
                total = o if total is None else total + o
            tops[d, c, h] = top
            sums[d, c, h] = total
        return carry

    lax.fori_loop(0, SIDE * (FW // 128), own_row, 0)
    for copy in [*later.values(), *query_later.values(), *sent]:
        copy.wait()


def exchange(keep_count, normed, w_qkv):
    dma = pltpu.SemaphoreType.DMA
    vmem = pl.BlockSpec(memory_space=pltpu.VMEM)
    shapes = [(SIDE, ROWS, 2 * FW)] * 3 + [(1, ROWS, 2 * LW)] * 3
    shapes += [(SIDE - 1, ROWS, 2 * LW), (SIDE, ROWS, GW)]
    return pl.pallas_call(
        exchange_kernel,
        out_shape=[jax.ShapeDtypeStruct(shape, jnp.bfloat16) for shape in shapes]
        + [jax.ShapeDtypeStruct((SIDE, FW // 128, 2, ROWS, 128), jnp.float32)] * 2,
        in_specs=[pl.BlockSpec(memory_space=pltpu.SMEM), vmem, pl.BlockSpec(memory_space=pltpu.HBM)],
        out_specs=[vmem] * 10,
        scratch_shapes=[
            pltpu.VMEM((len(BLOCKS), D, GW), jnp.bfloat16),
            pltpu.VMEM((SIDE, ROWS, 2 * FW), jnp.bfloat16),
            pltpu.VMEM((SIDE, ROWS, 2 * LW), jnp.bfloat16),
            pltpu.VMEM((SIDE, ROWS, GW), jnp.bfloat16),
            dma((len(BLOCKS),)),
            *[dma((SIDE,))] * 8,
            dma((2, SIDE)),
            dma((2, SIDE)),
            dma((2,)),
            dma((2,)),
        ],
        compiler_params=pltpu.CompilerParams(
            collective_id=0, has_side_effects=True, vmem_limit_bytes=36 * 2**20
        ),
        name="exchange",
    )(keep_count, normed, w_qkv)


def attend_kernel(start, pairs, begun, keep, q, *refs):
    if begun:
        below, above, tops, sums = refs[:4]
        sources = ((0, below), (2, above))
    else:
        sources = tuple((k, refs[2 * k : 2 * k + 2]) for k in range(3))
    out, live, keys, vals, masked, s0, s1, m0, m1, acc = refs[4 if begun else 6 :]
    y, x = place()
    for k, (dy, _) in enumerate(sources):
        for frame in range(SIDE):
            live[k * SIDE + frame] = keep[((y + SIDE - 1 + dy) % SIDE) * SIDE + frame]
    low = lax.broadcasted_iota(jnp.int32, (1, 128), 1) < HEAD_DIM
    one = jnp.ones((BLK, 128), jnp.bfloat16)
    counts = live
    total = 0
    for k, (_, kv) in enumerate(sources):

        def pack(slot, at, k=k, kv=kv):
            frame, block = slot // MOSTB, slot % MOSTB
            back = (x + SIDE - frame) % SIDE
            used = block < counts[k * SIDE + frame]

            def put(kv, back):
                rows = pl.ds(pl.multiple_of(block * BLK, BLK), BLK)
                to = pl.ds(pl.multiple_of(at * BLK, BLK), BLK)
                for c in range(pairs):
                    keys[c, to, :] = kv[back, rows, c * 128 : (c + 1) * 128]
                    v = kv[back, rows, (pairs + c) * 128 : (pairs + c + 1) * 128]
                    vals[c, 0, to, :] = jnp.where(low, v, one)
                    vals[c, 1, to, :] = jnp.where(low, one, v)

            if begun:
                pl.when(used)(lambda: put(kv, back))
            else:
                pl.when(used & (back == 0))(lambda: put(kv[0], 0))
                pl.when(used & (back > 0))(lambda: put(kv[1], back - 1))

            return at + used.astype(jnp.int32)

        total = lax.fori_loop(0, SIDE * MOSTB, pack, total)
    tail = pl.ds(pl.multiple_of(total * BLK, BLK), CH)
    for c in range(pairs):
        keys[c, tail, :] = jnp.zeros((CH, 128), jnp.bfloat16)
        for h in range(2):
            vals[c, h, tail, :] = jnp.zeros((CH, 128), jnp.bfloat16)

    def frame_rows(d, first, blocks, rows):
        full, left = blocks // (CH // BLK), blocks % (CH // BLK)
        for c in range(pairs):
            value = q[d, 0:rows, (start + c) * 128 : (start + c + 1) * 128]
            zero = jnp.zeros_like(value)
            masked[2 * c, 0:rows, :] = jnp.where(low, value, zero)
            masked[2 * c + 1, 0:rows, :] = jnp.where(low, zero, value)

        def span(j, width):
            return (
                pl.ds(pl.multiple_of(first * BLK + j * CH, BLK), width),
                pl.ds(pl.multiple_of(j * CH, BLK), width),
            )

        def score(c, j, width, partial, s, m):
            at, cols = span(j, width)
            for h in range(2):
                value = lax.dot_general(
                    masked[2 * c + h, 0:rows, :], keys[c, at, :],
                    (((1,), (1,)), ((), ())), preferred_element_type=jnp.float32,
                )
                if partial:
                    col = lax.broadcasted_iota(jnp.int32, (1, width), 1)
                    value = jnp.where(col < left * BLK, value, -1e30)
                s[h, 0:rows, cols] = value
                top = m[h, 0:rows, :]
                for t in range(width // 128):
                    top = jnp.maximum(top, value[:, t * 128 : (t + 1) * 128])
                m[h, 0:rows, :] = top

        def weigh(c, j, width, s, m):
            at, cols = span(j, width)
            for h in range(2):
                top = jnp.concatenate([m[h, 0:rows, :]] * (width // 128), axis=1)
                p = jnp.exp2(s[h, 0:rows, cols] - top).astype(jnp.bfloat16)
                acc[h, 0:rows, :] += jnp.dot(p, vals[c, h, at, :], preferred_element_type=jnp.float32)

        bufs = ((s0, m0), (s1, m1))
        for stage in range(pairs + 1):
            s, m = bufs[(stage + 1) % 2]
            sn, mn = bufs[stage % 2]
            if stage:
                top = jnp.broadcast_to(
                    jnp.max(m[:, 0:rows, :], axis=2, keepdims=True), (2, rows, 128)
                )
                if begun:
                    before = tops[d, stage - 1, :, 0:rows, :]
                    top = jnp.maximum(top, before)
                    acc[:, 0:rows, :] = sums[d, stage - 1, :, 0:rows, :] * jnp.exp2(before - top)
                else:
                    acc[:, 0:rows, :] = jnp.zeros((2, rows, 128), jnp.float32)
                m[:, 0:rows, :] = top
            if stage < pairs:
                mn[:, 0:rows, :] = jnp.full((2, rows, 128), -1e30, jnp.float32)

            def step(j, width, partial, stage=stage, s=s, m=m, sn=sn, mn=mn):
                if stage < pairs:
                    score(stage, j, width, partial, sn, mn)
                if stage:
                    weigh(stage - 1, j, width, s, m)

            lax.fori_loop(0, full, lambda j, t, step=step: (step(j, CH, False), t)[1], 0)

            @pl.when((left > 0) & (left <= CH // BLK // 2))
            def _(step=step):
                step(full, CH // 2, True)

            @pl.when(left > CH // BLK // 2)
            def _(step=step):
                step(full, CH, True)

            if stage:
                even, odd = acc[0, 0:rows, :], acc[1, 0:rows, :]
                even = even / pltpu.roll(even, HEAD_DIM, 1)
                odd = odd / pltpu.roll(odd, HEAD_DIM, 1)
                out[d, 0:rows, (stage - 1) * 128 : stage * 128] = jnp.where(low, even, odd).astype(jnp.bfloat16)

    def frame_body(f, first):
        blocks = counts[f]
        for k in range(1, len(sources) * SIDE - SIDE + 1):
            blocks += counts[f + k]
        own = keep[y * SIDE + f]
        d = (x + SIDE - f) % SIDE
        for n in range(1, MOSTB + 1):

            @pl.when(own == n)
            def _(n=n):
                frame_rows(d, first, blocks, n * BLK)
                if n < MOSTB:
                    out[d, n * BLK :, :] = jnp.zeros((ROWS - n * BLK, pairs * 128), jnp.bfloat16)

        return first + counts[f]

    lax.fori_loop(0, SIDE, frame_body, 0)


def attend(start, pairs, begun, keep_count, q, *rest):
    window = BEGUN_WINDOW if begun else WINDOW
    vmem = pl.BlockSpec(memory_space=pltpu.VMEM)
    return pl.pallas_call(
        functools.partial(attend_kernel, start, pairs, begun),
        out_shape=jax.ShapeDtypeStruct((SIDE, ROWS, pairs * 128), jnp.bfloat16),
        in_specs=[pl.BlockSpec(memory_space=pltpu.SMEM)] + [vmem] * (1 + len(rest)),
        out_specs=vmem,
        scratch_shapes=[
            pltpu.SMEM((3 * SIDE,), jnp.int32),
            pltpu.VMEM((pairs, KROWS, 128), jnp.bfloat16),
            pltpu.VMEM((pairs, 2, KROWS, 128), jnp.bfloat16),
            pltpu.VMEM((2 * pairs, ROWS, 128), jnp.bfloat16),
            pltpu.VMEM((2, ROWS, window), jnp.float32),
            pltpu.VMEM((2, ROWS, window), jnp.float32),
            *[pltpu.VMEM((2, ROWS, 128), jnp.float32)] * 3,
        ],
        compiler_params=pltpu.CompilerParams(vmem_limit_bytes=(32 if begun else 36) * 2**20),
        cost_estimate=pl.CostEstimate(
            flops=pairs * 18 * 10**9, bytes_accessed=pairs * 2**21, transcendentals=0
        ),
        name="attend",
    )(keep_count, q, *rest)


def project_kernel(own, one, two, three, rest, w, out, got, most, few, total, wsem, ss, rs):
    y, x = place()
    barrier = pltpu.get_barrier_semaphore()
    for delta in (1, 2, 3):
        pl.semaphore_signal(barrier, inc=1, device_id=device(y, x + delta), device_id_type=MESH)
    loads = []
    for delta in range(SIDE):
        group = ((x + SIDE - delta) % SIDE) * GW
        for k, (skip, size, to) in enumerate(((0, FW, most), (FW, LW, few))):
            rows = pl.ds(pl.multiple_of(group + skip, LW), size)
            load = pltpu.make_async_copy(w.at[rows, :], to.at[pl.ds(delta * size, size), :], wsem.at[k, delta])
            load.start()
            loads.append(load)
    pl.semaphore_wait(barrier, 3)
    copies = []
    for delta in (2, 1, 3):
        copy = pltpu.make_async_remote_copy(
            rest.at[(SIDE - delta) % SIDE], got.at[delta], ss.at[delta], rs.at[delta],
            device_id=device(y, x + delta), device_id_type=MESH,
        )
        copy.start()
        copies.append(copy)
    for load in loads:
        load.wait()
    tile = 512

    def first(t, carry):
        cols = pl.ds(pl.multiple_of(t * tile, 128), tile)
        left = jnp.concatenate([own[...], one[...], two[...], three[...], rest[0]], axis=1)
        right = jnp.concatenate([most[:, cols], few[0:LW, cols]], axis=0)
        total[:, cols] = jnp.dot(left, right, preferred_element_type=jnp.float32)
        return carry

    lax.fori_loop(0, D // tile, first, 0)
    for copy in copies:
        copy.wait()

    def second(t, square):
        cols = pl.ds(pl.multiple_of(t * tile, 128), tile)
        left = jnp.concatenate([got[1], got[2], got[3]], axis=1)
        value = total[:, cols] + jnp.dot(left, few[LW:, cols], preferred_element_type=jnp.float32)
        total[:, cols] = value
        for k in range(tile // 128):
            piece = value[:, k * 128 : (k + 1) * 128]
            square += piece * piece
        return square

    square = lax.fori_loop(0, D // tile, second, jnp.zeros((ROWS, 128), jnp.float32))
    scale = lax.rsqrt(jnp.sum(square, axis=1, keepdims=True) / D + 1e-06)
    scale = jnp.broadcast_to(scale, (ROWS, 128))
    for k in range(D // 128):
        cols = slice(k * 128, (k + 1) * 128)
        out[:, cols] = (total[:, cols] * scale).astype(jnp.bfloat16)


def project(parts, rest, w_out):
    dma = pltpu.SemaphoreType.DMA
    vmem = pl.BlockSpec(memory_space=pltpu.VMEM)
    return pl.pallas_call(
        project_kernel,
        out_shape=jax.ShapeDtypeStruct((ROWS, D), jnp.bfloat16),
        in_specs=[vmem] * 5 + [pl.BlockSpec(memory_space=pltpu.HBM)],
        out_specs=vmem,
        scratch_shapes=[
            pltpu.VMEM((SIDE, ROWS, LW), jnp.bfloat16),
            pltpu.VMEM((SIDE * FW, D), jnp.bfloat16),
            pltpu.VMEM((SIDE * LW, D), jnp.bfloat16),
            pltpu.VMEM((ROWS, D), jnp.float32),
            dma((2, SIDE)),
            dma((SIDE,)),
            dma((SIDE,)),
        ],
        compiler_params=pltpu.CompilerParams(
            collective_id=1, has_side_effects=True, vmem_limit_bytes=24 * 2**20
        ),
        name="project",
    )(*parts, rest, w_out)


def scatter_kernel(order, count, block, out, zero, sems):
    own = count[lax.axis_index("frame")]
    zero[...] = jnp.zeros_like(zero)

    def each(act):
        for j in range(order.shape[1]):
            rows = pl.ds(pl.multiple_of(order[0, j] * BLK, BLK), BLK)
            if j == MOSTB:
                act(pltpu.make_async_copy(zero, out.at[rows, :], sems.at[j]))
                continue

            @pl.when(j < own)
            def _(j=j, rows=rows):
                act(pltpu.make_async_copy(block.at[pl.ds(j * BLK, BLK), :], out.at[rows, :], sems.at[j]))

            @pl.when(j >= own)
            def _(j=j, rows=rows):
                act(pltpu.make_async_copy(zero, out.at[rows, :], sems.at[j]))

    each(lambda copy: copy.start())
    each(lambda copy: copy.wait())


def scatter(keep_order, keep_count, normalized):
    blocks = keep_order.shape[1]
    smem = pl.BlockSpec(memory_space=pltpu.SMEM)
    return pl.pallas_call(
        scatter_kernel,
        in_specs=[smem, smem, pl.BlockSpec(memory_space=pltpu.VMEM)],
        out_specs=pl.BlockSpec(memory_space=pl.ANY),
        out_shape=jax.ShapeDtypeStruct((blocks * BLK, D), jnp.bfloat16),
        scratch_shapes=[pltpu.VMEM((BLK, D), jnp.bfloat16), pltpu.SemaphoreType.DMA((blocks,))],
        compiler_params=pltpu.CompilerParams(vmem_limit_bytes=8 * 2**20),
        name="scatter",
    )(keep_order, keep_count, normalized)


def shifted(value, dy, dx):
    def to(f):
        return (f // SIDE + dy) % SIDE * SIDE + (f + dx) % SIDE

    return lax.ppermute(value, "frame", [(f, to(f)) for f in range(SIDE * SIDE)])


def shards(tokens, keep_count, keep_order, w_qkv, w_out):
    normed = norm_kept(keep_order, tokens)
    below, row, above, *mine, last, q, tops, sums = exchange(keep_count, normed, w_qkv)
    last_below = shifted(last, 1, 0)
    last_above = shifted(last, -1, 0)
    part = attend(0, 2, True, keep_count, q, below, above, tops, sums)
    parts = [shifted(part[(SIDE - dx) % SIDE], 0, dx) if dx else part[0] for dx in range(SIDE)]
    rest = attend(2, 1, False, keep_count, q, mine[0], last_below, mine[1], last, mine[2], last_above)
    normalized = project(parts, rest, w_out)
    return scatter(keep_order, keep_count, normalized)


def solution(mesh):
    return jax.shard_map(
        shards,
        mesh=mesh,
        in_specs=(P(("orbit", "frame"), None), P("orbit"), P(("orbit", "frame"), None), P(), P()),
        out_specs=P(("orbit", "frame"), None),
        check_vma=False,
    )
```

```python
import functools

import jax
import jax.numpy as jnp
from jax import lax
from jax.experimental import pallas as pl
from jax.experimental.pallas import tpu as pltpu
from jax.sharding import PartitionSpec as P

D = 1536
HEADS = 24
HEAD_DIM = 64
BLK = 128
MOSTB = 3
ROWS = MOSTB * BLK
SIDE = 4
GW = 384
CH = 1024
WINDOW = 28 * BLK
BEGUN_WINDOW = 16 * BLK
KROWS = 36 * BLK + CH
SCALE = HEAD_DIM ** (-0.5) * 1.4426950408889634
MESH = pl.DeviceIdType.MESH


def place():
    me = lax.axis_index("frame")
    return me // SIDE, me % SIDE


def device(y, x):
    return {"frame": (y % SIDE) * SIDE + x % SIDE}


def norm_kernel(order, tokens, out):
    for j in range(MOSTB):
        rows = pl.ds(pl.multiple_of(order[0, j] * BLK, BLK), BLK)
        wide = tokens[rows, :].astype(jnp.float32)
        scale = lax.rsqrt(jnp.mean(wide * wide, axis=-1, keepdims=True) + 1e-06)
        out[j * BLK : (j + 1) * BLK, :] = (wide * scale).astype(jnp.bfloat16)


def norm_kept(keep_order, tokens):
    vmem = pl.BlockSpec(memory_space=pltpu.VMEM)
    return pl.pallas_call(
        norm_kernel,
        in_specs=[pl.BlockSpec(memory_space=pltpu.SMEM), vmem],
        out_specs=vmem,
        out_shape=jax.ShapeDtypeStruct((ROWS, D), jnp.bfloat16),
        compiler_params=pltpu.CompilerParams(vmem_limit_bytes=12 * 2**20),
        name="norm_kept",
    )(keep_order, tokens)


BLOCKS = ((1, 1), (1, 2), (0, 1), (0, 2), (3, 1), (3, 2), (2, 1), (2, 2), (1, 0), (3, 0), (2, 0), (0, 0))
FW = 256
LW = GW - FW


def exchange_kernel(
    keep, normed, w, below, row, above, mine_below, mine, mine_above, last, q, tops, sums,
    wbuf, kvs, lasts, qs, wsem, xs, xr, ls, lr, qss, qsr, rss, rsr, ys, yr, ms, mr,
):
    y, x = place()
    loads = []
    for i, (delta, kind) in enumerate(BLOCKS):
        col = pl.multiple_of(kind * (HEADS * HEAD_DIM) + ((x + delta) % SIDE) * GW, 128)
        load = pltpu.make_async_copy(w.at[:, pl.ds(col, GW)], wbuf.at[i], wsem.at[i])
        load.start()
        loads.append(load)
    barrier = pltpu.get_barrier_semaphore()
    peers = [(0, 1), (0, 2), (0, 3), (1, 0), (3, 0)]
    for dy, dx in peers:
        pl.semaphore_signal(barrier, inc=1, device_id=device(y + dy, x + dx), device_id_type=MESH)

    def product(i, put):
        loads[i].wait()

        def rows(r, carry):
            at = pl.ds(pl.multiple_of(r * BLK, BLK), BLK)
            value = jnp.dot(normed[at, :], wbuf[i], preferred_element_type=jnp.float32)
            put(at, value)
            return carry

        lax.fori_loop(0, MOSTB, rows, 0)

    def across(src, dst, send, recv, delta):
        return pltpu.make_async_remote_copy(
            src.at[delta], dst.at[delta], send.at[delta], recv.at[delta],
            device_id=device(y, x + delta), device_id_type=MESH,
        )

    first = {delta: across(kvs, row, xs, xr, delta) for delta in (1, 2, 3)}
    later = {
        delta: pltpu.make_async_remote_copy(
            lasts.at[delta], last.at[delta - 1], ls.at[delta], lr.at[delta],
            device_id=device(y, x + delta), device_id_type=MESH,
        )
        for delta in (1, 2, 3)
    }
    part, rest = (slice(None), slice(None), pl.ds(0, FW)), (slice(None), slice(None), pl.ds(FW, LW))
    query = {delta: across(qs.at[part], q.at[part], qss, qsr, delta) for delta in (1, 2, 3)}
    query_later = {delta: across(qs.at[rest], q.at[rest], rss, rsr, delta) for delta in (1, 2, 3)}
    sent = []

    def up_down(delta):
        for way, (dy, to) in enumerate(((1, below), (-1, above))):
            copy = pltpu.make_async_remote_copy(
                row.at[delta], to.at[delta], ys.at[way, delta], yr.at[way, delta],
                device_id=device(y + dy, x), device_id_type=MESH,
            )
            copy.start()
            sent.append(copy)

    for i, (delta, kind) in enumerate(BLOCKS):
        if kind == 0:
            to = q if delta == 0 else qs

            def put(at, value, delta=delta, to=to):
                to[delta, at, :] = (value * SCALE).astype(jnp.bfloat16)
        else:
            to, rest = (row, mine) if delta == 0 else (kvs, lasts)

            def put(at, value, delta=delta, kind=kind, to=to, rest=rest):
                value = value.astype(jnp.bfloat16)
                to[delta, at, pl.ds((kind - 1) * FW, FW)] = value[:, :FW]
                rest[delta, at, pl.ds((kind - 1) * LW, LW)] = value[:, FW:]

        product(i, put)
        if i == 1:
            pl.semaphore_wait(barrier, len(peers))
        if kind == 2:
            if delta == 0:
                up_down(0)
                for way, (dy, to) in enumerate(((1, mine_below), (-1, mine_above))):
                    copy = pltpu.make_async_remote_copy(
                        mine, to, ms.at[way], mr.at[way],
                        device_id=device(y + dy, x), device_id_type=MESH,
                    )
                    copy.start()
                    sent.append(copy)
            else:
                first[delta].start()
    first[1].wait()
    up_down(1)
    first[3].wait()
    up_down(3)
    for delta in (1, 3, 2):
        query[delta].start()
    first[2].wait()
    up_down(2)
    for delta in (1, 3, 2):
        later[delta].start()
    for delta in (1, 3, 2):
        query_later[delta].start()
    live = [keep[y * SIDE + (x + SIDE - back) % SIDE] * BLK for back in range(SIDE)]
    low = lax.broadcasted_iota(jnp.int32, (1, 128), 1) < HEAD_DIM
    col = lax.broadcasted_iota(jnp.int32, (1, ROWS), 1)
    ones = jnp.ones((ROWS, 128), jnp.bfloat16)

    def own_row(i, carry):
        d, c = i // (FW // 128), i % (FW // 128)

        @pl.when((d > 0) & (c == 0))
        def _():
            across(qs.at[part], q.at[part], qss, qsr, d).wait()

        at = pl.ds(pl.multiple_of(c * 128, 128), 128)
        value_at = pl.ds(pl.multiple_of(FW + c * 128, 128), 128)
        masks = (low, jnp.logical_not(low))
        query_pair = q[d, :, at]
        scores, highest = [], []
        for h in range(2):
            value = jnp.where(masks[h], query_pair, jnp.zeros_like(query_pair))
            rowed = []
            top = None
            for back in range(SIDE):
                score = lax.dot_general(
                    value, row[back, :, at], (((1,), (1,)), ((), ())),
                    preferred_element_type=jnp.float32,
                )
                score = jnp.where(col < live[back], score, -1e30)
                rowed.append(score)
                for t in range(MOSTB):
                    piece = score[:, t * 128 : (t + 1) * 128]
                    top = piece if top is None else jnp.maximum(top, piece)
            scores.append(rowed)
            highest.append(top)
        for h in range(2):
            top = jnp.broadcast_to(jnp.max(highest[h], axis=1, keepdims=True), (ROWS, 128))
            wide = jnp.concatenate([top] * MOSTB, axis=1)
            total = None
            for back in range(SIDE):
                p = jnp.exp2(scores[h][back] - wide).astype(jnp.bfloat16)
                v = jnp.where(masks[h], row[back, :, value_at], ones)
                o = jnp.dot(p, v, preferred_element_type=jnp.float32)
                total = o if total is None else total + o
            tops[d, c, h] = top
            sums[d, c, h] = total
        return carry

    lax.fori_loop(0, SIDE * (FW // 128), own_row, 0)
    for copy in [*later.values(), *query_later.values(), *sent]:
        copy.wait()


def exchange(keep_count, normed, w_qkv):
    dma = pltpu.SemaphoreType.DMA
    vmem = pl.BlockSpec(memory_space=pltpu.VMEM)
    shapes = [(SIDE, ROWS, 2 * FW)] * 3 + [(1, ROWS, 2 * LW)] * 3
    shapes += [(SIDE - 1, ROWS, 2 * LW), (SIDE, ROWS, GW)]
    return pl.pallas_call(
        exchange_kernel,
        out_shape=[jax.ShapeDtypeStruct(shape, jnp.bfloat16) for shape in shapes]
        + [jax.ShapeDtypeStruct((SIDE, FW // 128, 2, ROWS, 128), jnp.float32)] * 2,
        in_specs=[pl.BlockSpec(memory_space=pltpu.SMEM), vmem, pl.BlockSpec(memory_space=pltpu.HBM)],
        out_specs=[vmem] * 10,
        scratch_shapes=[
            pltpu.VMEM((len(BLOCKS), D, GW), jnp.bfloat16),
            pltpu.VMEM((SIDE, ROWS, 2 * FW), jnp.bfloat16),
            pltpu.VMEM((SIDE, ROWS, 2 * LW), jnp.bfloat16),
            pltpu.VMEM((SIDE, ROWS, GW), jnp.bfloat16),
            dma((len(BLOCKS),)),
            *[dma((SIDE,))] * 8,
            dma((2, SIDE)),
            dma((2, SIDE)),
            dma((2,)),
            dma((2,)),
        ],
        compiler_params=pltpu.CompilerParams(
            collective_id=0, has_side_effects=True, vmem_limit_bytes=36 * 2**20
        ),
        name="exchange",
    )(keep_count, normed, w_qkv)


def attend_kernel(start, pairs, begun, keep, q, *refs):
    if begun:
        below, above, tops, sums = refs[:4]
        sources = ((0, below), (2, above))
    else:
        sources = tuple((k, refs[2 * k : 2 * k + 2]) for k in range(3))
    out, live, keys, vals, masked, s0, s1, m0, m1, acc = refs[4 if begun else 6 :]
    y, x = place()
    for k, (dy, _) in enumerate(sources):
        for frame in range(SIDE):
            live[k * SIDE + frame] = keep[((y + SIDE - 1 + dy) % SIDE) * SIDE + frame]
    low = lax.broadcasted_iota(jnp.int32, (1, 128), 1) < HEAD_DIM
    one = jnp.ones((BLK, 128), jnp.bfloat16)
    counts = live
    total = 0
    for k, (_, kv) in enumerate(sources):

        def pack(frame, at, k=k, kv=kv):
            back = (x + SIDE - frame) % SIDE
            used = counts[k * SIDE + frame]

            def put(kv, back):
                def block(i, carry):
                    rows = pl.ds(pl.multiple_of(i * BLK, BLK), BLK)
                    to = pl.ds(pl.multiple_of((at + i) * BLK, BLK), BLK)
                    for c in range(pairs):
                        keys[c, to, :] = kv[back, rows, c * 128 : (c + 1) * 128]
                        v = kv[back, rows, (pairs + c) * 128 : (pairs + c + 1) * 128]
                        vals[c, 0, to, :] = jnp.where(low, v, one)
                        vals[c, 1, to, :] = jnp.where(low, one, v)
                    return carry

                lax.fori_loop(0, used, block, 0)

            if begun:
                put(kv, back)
            else:
                pl.when(back == 0)(lambda: put(kv[0], 0))
                pl.when(back > 0)(lambda: put(kv[1], back - 1))

            return at + used

        total = lax.fori_loop(0, SIDE, pack, total)
    tail = pl.ds(pl.multiple_of(total * BLK, BLK), CH)
    for c in range(pairs):
        keys[c, tail, :] = jnp.zeros((CH, 128), jnp.bfloat16)
        for h in range(2):
            vals[c, h, tail, :] = jnp.zeros((CH, 128), jnp.bfloat16)

    def frame_rows(d, first, blocks, rows):
        full, left = blocks // (CH // BLK), blocks % (CH // BLK)
        for c in range(pairs):
            value = q[d, 0:rows, (start + c) * 128 : (start + c + 1) * 128]
            zero = jnp.zeros_like(value)
            masked[2 * c, 0:rows, :] = jnp.where(low, value, zero)
            masked[2 * c + 1, 0:rows, :] = jnp.where(low, zero, value)

        def span(j, width):
            return (
                pl.ds(pl.multiple_of(first * BLK + j * CH, BLK), width),
                pl.ds(pl.multiple_of(j * CH, BLK), width),
            )

        def score(c, j, width, partial, s, m):
            at, cols = span(j, width)
            for h in range(2):
                value = lax.dot_general(
                    masked[2 * c + h, 0:rows, :], keys[c, at, :],
                    (((1,), (1,)), ((), ())), preferred_element_type=jnp.float32,
                )
                if partial:
                    col = lax.broadcasted_iota(jnp.int32, (1, width), 1)
                    value = jnp.where(col < left * BLK, value, -1e30)
                s[h, 0:rows, cols] = value
                top = m[h, 0:rows, :]
                for t in range(width // 128):
                    top = jnp.maximum(top, value[:, t * 128 : (t + 1) * 128])
                m[h, 0:rows, :] = top

        def weigh(c, j, width, s, m):
            at, cols = span(j, width)
            for h in range(2):
                top = jnp.concatenate([m[h, 0:rows, :]] * (width // 128), axis=1)
                p = jnp.exp2(s[h, 0:rows, cols] - top).astype(jnp.bfloat16)
                acc[h, 0:rows, :] += jnp.dot(p, vals[c, h, at, :], preferred_element_type=jnp.float32)

        bufs = ((s0, m0), (s1, m1))
        for stage in range(pairs + 1):
            s, m = bufs[(stage + 1) % 2]
            sn, mn = bufs[stage % 2]
            if stage:
                top = jnp.broadcast_to(
                    jnp.max(m[:, 0:rows, :], axis=2, keepdims=True), (2, rows, 128)
                )
                if begun:
                    before = tops[d, stage - 1, :, 0:rows, :]
                    top = jnp.maximum(top, before)
                    acc[:, 0:rows, :] = sums[d, stage - 1, :, 0:rows, :] * jnp.exp2(before - top)
                else:
                    acc[:, 0:rows, :] = jnp.zeros((2, rows, 128), jnp.float32)
                m[:, 0:rows, :] = top
            if stage < pairs:
                mn[:, 0:rows, :] = jnp.full((2, rows, 128), -1e30, jnp.float32)

            def step(j, width, partial, stage=stage, s=s, m=m, sn=sn, mn=mn):
                if stage < pairs:
                    score(stage, j, width, partial, sn, mn)
                if stage:
                    weigh(stage - 1, j, width, s, m)

            lax.fori_loop(0, full, lambda j, t, step=step: (step(j, CH, False), t)[1], 0)

            @pl.when((left > 0) & (left <= CH // BLK // 2))
            def _(step=step):
                step(full, CH // 2, True)

            @pl.when(left > CH // BLK // 2)
            def _(step=step):
                step(full, CH, True)

            if stage:
                even, odd = acc[0, 0:rows, :], acc[1, 0:rows, :]
                even = even / pltpu.roll(even, HEAD_DIM, 1)
                odd = odd / pltpu.roll(odd, HEAD_DIM, 1)
                out[d, 0:rows, (stage - 1) * 128 : stage * 128] = jnp.where(low, even, odd).astype(jnp.bfloat16)

    def frame_body(f, first):
        blocks = counts[f]
        for k in range(1, len(sources) * SIDE - SIDE + 1):
            blocks += counts[f + k]
        own = keep[y * SIDE + f]
        d = (x + SIDE - f) % SIDE
        for n in range(1, MOSTB + 1):

            @pl.when(own == n)
            def _(n=n):
                frame_rows(d, first, blocks, n * BLK)
                if n < MOSTB:
                    out[d, n * BLK :, :] = jnp.zeros((ROWS - n * BLK, pairs * 128), jnp.bfloat16)

        return first + counts[f]

    lax.fori_loop(0, SIDE, frame_body, 0)


def attend(start, pairs, begun, keep_count, q, *rest):
    window = BEGUN_WINDOW if begun else WINDOW
    vmem = pl.BlockSpec(memory_space=pltpu.VMEM)
    return pl.pallas_call(
        functools.partial(attend_kernel, start, pairs, begun),
        out_shape=jax.ShapeDtypeStruct((SIDE, ROWS, pairs * 128), jnp.bfloat16),
        in_specs=[pl.BlockSpec(memory_space=pltpu.SMEM)] + [vmem] * (1 + len(rest)),
        out_specs=vmem,
        scratch_shapes=[
            pltpu.SMEM((3 * SIDE,), jnp.int32),
            pltpu.VMEM((pairs, KROWS, 128), jnp.bfloat16),
            pltpu.VMEM((pairs, 2, KROWS, 128), jnp.bfloat16),
            pltpu.VMEM((2 * pairs, ROWS, 128), jnp.bfloat16),
            pltpu.VMEM((2, ROWS, window), jnp.float32),
            pltpu.VMEM((2, ROWS, window), jnp.float32),
            *[pltpu.VMEM((2, ROWS, 128), jnp.float32)] * 3,
        ],
        compiler_params=pltpu.CompilerParams(vmem_limit_bytes=(32 if begun else 36) * 2**20),
        cost_estimate=pl.CostEstimate(
            flops=pairs * 18 * 10**9, bytes_accessed=pairs * 2**21, transcendentals=0
        ),
        name="attend",
    )(keep_count, q, *rest)


def project_kernel(own, one, two, three, rest, w, out, got, most, few, total, wsem, ss, rs):
    y, x = place()
    barrier = pltpu.get_barrier_semaphore()
    for delta in (1, 2, 3):
        pl.semaphore_signal(barrier, inc=1, device_id=device(y, x + delta), device_id_type=MESH)
    loads = []
    for delta in range(SIDE):
        group = ((x + SIDE - delta) % SIDE) * GW
        for k, (skip, size, to) in enumerate(((0, FW, most), (FW, LW, few))):
            rows = pl.ds(pl.multiple_of(group + skip, LW), size)
            load = pltpu.make_async_copy(w.at[rows, :], to.at[pl.ds(delta * size, size), :], wsem.at[k, delta])
            load.start()
            loads.append(load)
    pl.semaphore_wait(barrier, 3)
    copies = []
    for delta in (2, 1, 3):
        copy = pltpu.make_async_remote_copy(
            rest.at[(SIDE - delta) % SIDE], got.at[delta], ss.at[delta], rs.at[delta],
            device_id=device(y, x + delta), device_id_type=MESH,
        )
        copy.start()
        copies.append(copy)
    for load in loads:
        load.wait()
    tile = 512

    def first(t, carry):
        cols = pl.ds(pl.multiple_of(t * tile, 128), tile)
        left = jnp.concatenate([own[...], one[...], two[...], three[...], rest[0]], axis=1)
        right = jnp.concatenate([most[:, cols], few[0:LW, cols]], axis=0)
        total[:, cols] = jnp.dot(left, right, preferred_element_type=jnp.float32)
        return carry

    lax.fori_loop(0, D // tile, first, 0)
    for copy in copies:
        copy.wait()

    def second(t, square):
        cols = pl.ds(pl.multiple_of(t * tile, 128), tile)
        left = jnp.concatenate([got[1], got[2], got[3]], axis=1)
        value = total[:, cols] + jnp.dot(left, few[LW:, cols], preferred_element_type=jnp.float32)
        total[:, cols] = value
        for k in range(tile // 128):
            piece = value[:, k * 128 : (k + 1) * 128]
            square += piece * piece
        return square

    square = lax.fori_loop(0, D // tile, second, jnp.zeros((ROWS, 128), jnp.float32))
    scale = lax.rsqrt(jnp.sum(square, axis=1, keepdims=True) / D + 1e-06)
    scale = jnp.broadcast_to(scale, (ROWS, 128))
    for k in range(D // 128):
        cols = slice(k * 128, (k + 1) * 128)
        out[:, cols] = (total[:, cols] * scale).astype(jnp.bfloat16)


def project(parts, rest, w_out):
    dma = pltpu.SemaphoreType.DMA
    vmem = pl.BlockSpec(memory_space=pltpu.VMEM)
    return pl.pallas_call(
        project_kernel,
        out_shape=jax.ShapeDtypeStruct((ROWS, D), jnp.bfloat16),
        in_specs=[vmem] * 5 + [pl.BlockSpec(memory_space=pltpu.HBM)],
        out_specs=vmem,
        scratch_shapes=[
            pltpu.VMEM((SIDE, ROWS, LW), jnp.bfloat16),
            pltpu.VMEM((SIDE * FW, D), jnp.bfloat16),
            pltpu.VMEM((SIDE * LW, D), jnp.bfloat16),
            pltpu.VMEM((ROWS, D), jnp.float32),
            dma((2, SIDE)),
            dma((SIDE,)),
            dma((SIDE,)),
        ],
        compiler_params=pltpu.CompilerParams(
            collective_id=1, has_side_effects=True, vmem_limit_bytes=24 * 2**20
        ),
        name="project",
    )(*parts, rest, w_out)


def scatter_kernel(order, count, block, out, zero, sems):
    own = count[lax.axis_index("frame")]
    zero[...] = jnp.zeros_like(zero)

    def each(act):
        for j in range(order.shape[1]):
            rows = pl.ds(pl.multiple_of(order[0, j] * BLK, BLK), BLK)
            if j == MOSTB:
                act(pltpu.make_async_copy(zero, out.at[rows, :], sems.at[j]))
                continue

            @pl.when(j < own)
            def _(j=j, rows=rows):
                act(pltpu.make_async_copy(block.at[pl.ds(j * BLK, BLK), :], out.at[rows, :], sems.at[j]))

            @pl.when(j >= own)
            def _(j=j, rows=rows):
                act(pltpu.make_async_copy(zero, out.at[rows, :], sems.at[j]))

    each(lambda copy: copy.start())
    each(lambda copy: copy.wait())


def scatter(keep_order, keep_count, normalized):
    blocks = keep_order.shape[1]
    smem = pl.BlockSpec(memory_space=pltpu.SMEM)
    return pl.pallas_call(
        scatter_kernel,
        in_specs=[smem, smem, pl.BlockSpec(memory_space=pltpu.VMEM)],
        out_specs=pl.BlockSpec(memory_space=pl.ANY),
        out_shape=jax.ShapeDtypeStruct((blocks * BLK, D), jnp.bfloat16),
        scratch_shapes=[pltpu.VMEM((BLK, D), jnp.bfloat16), pltpu.SemaphoreType.DMA((blocks,))],
        compiler_params=pltpu.CompilerParams(vmem_limit_bytes=8 * 2**20),
        name="scatter",
    )(keep_order, keep_count, normalized)


def shifted(value, dy, dx):
    def to(f):
        return (f // SIDE + dy) % SIDE * SIDE + (f + dx) % SIDE

    return lax.ppermute(value, "frame", [(f, to(f)) for f in range(SIDE * SIDE)])


def shards(tokens, keep_count, keep_order, w_qkv, w_out):
    normed = norm_kept(keep_order, tokens)
    below, row, above, *mine, last, q, tops, sums = exchange(keep_count, normed, w_qkv)
    last_below = shifted(last, 1, 0)
    last_above = shifted(last, -1, 0)
    part = attend(0, 2, True, keep_count, q, below, above, tops, sums)
    parts = [shifted(part[(SIDE - dx) % SIDE], 0, dx) if dx else part[0] for dx in range(SIDE)]
    rest = attend(2, 1, False, keep_count, q, mine[0], last_below, mine[1], last, mine[2], last_above)
    normalized = project(parts, rest, w_out)
    return scatter(keep_order, keep_count, normalized)


def solution(mesh):
    return jax.shard_map(
        shards,
        mesh=mesh,
        in_specs=(P(("orbit", "frame"), None), P("orbit"), P(("orbit", "frame"), None), P(), P()),
        out_specs=P(("orbit", "frame"), None),
        check_vma=False,
    )
```
